32 devices in a mesh: row: 4 (over z), col: 8 (over y, x, core).
Axes of the slice: x: 2, y: 2, z: 4, core: 2. Of those that a mesh axis runs over, the one named last changes fastest.
Arguments:
- density: float32 [1024, 1024], P('row', 'col'), may hold values from -0.21875 to 0.21875
- hamiltonian: float32 [1024, 1024], P('row', 'col'), may hold values from -6 to 6
- block_mask: int32 [8, 8], replicated, may hold values from 0 to 1, as said below
Outputs:
- hp_product: float32 [1024, 1024], P('row', 'col')
- php_product: float32 [1024, 1024], P('row', 'col')
- gradient: float32 [1024, 1024], P('row', 'col')
The draws below stay inside these ranges and needn't reach their ends.
Inputs may be any that keep to these rules, and one draw needn't show every extreme that they name: block_mask is symmetric with ones on the diagonal.
All inputs are finite; a program needn't handle non-finite values.
Results may differ from the reference program's by a relative error of at most 0.000098.
Values sent between devices are 32-bit elements; how exact they have to be, the bound alone decides.
No kernel may reach another device: no remote copies, remote signals or barrier semaphores. Data moves between devices by JAX's collectives and lax.ppermute only.
A program may use at most 64 MiB of HBM per device.

```python
import jax
import jax.numpy as jnp
from jax import lax

BLK = 128
NORB = 1024
NB = 8


def draw_block_mask(key, part):
    spots = jax.random.randint(key, (NB, 3), 0, 5)
    offset = jnp.abs(spots[:, None, :] - spots[None, :, :])
    wrapped = jnp.minimum(offset, 5 - offset)
    nearby = jnp.all(wrapped <= 1, axis=-1)
    return nearby.astype(jnp.int32)


def levels(key, extent, pieces, least, top_value):
    factor_of, own = 1.0, jax.random.fold_in(key, 6)
    for dim, shards_of in pieces:
        heights = jnp.exp(jax.random.uniform(jax.random.fold_in(own, dim), (shards_of,), jnp.float32, least / len(pieces), top_value / len(pieces)))
        factor_of = factor_of * jnp.repeat(heights, extent[dim] // shards_of).reshape([-1 if axis == dim else 1 for axis in range(len(extent))])
    return factor_of


def scatter_about(own_key, dims, scale, most, shards=(), dtype=jnp.bfloat16):
    values = scale * jax.random.normal(own_key, dims, jnp.float32)
    if shards:
        values = values * levels(own_key, dims, shards, -0.22, 0.18)
    return jnp.clip(values, -most, most).astype(dtype)


def setup_inputs(seed: int = 0) -> dict:
    key_list = jax.random.split(jax.random.key(seed), 4)
    return {
        "density": scatter_about(key_list[0], (NORB, NORB), (6 * BLK) ** -0.5, 0.21875, ((0, 4), (1, 8)), jnp.float32),
        "hamiltonian": scatter_about(key_list[1], (NORB, NORB), 1.0, 6.0, ((0, 4), (1, 8)), jnp.float32),
        "block_mask": draw_block_mask(jax.random.fold_in(key_list[3], 71), 0),
    }


def reference(density, hamiltonian, block_mask):
    pattern = jnp.repeat(jnp.repeat(block_mask.astype(jnp.float32), BLK, axis=0), BLK, axis=1)
    kept_density = density * pattern
    kept_hamiltonian = hamiltonian * pattern

    def masked_product(leading, second):
        return jnp.dot(leading, second, precision=lax.Precision.HIGHEST, preferred_element_type=jnp.float32) * pattern

    hp_product = masked_product(kept_hamiltonian, kept_density)
    ph_product = masked_product(kept_density, kept_hamiltonian)
    php_product = masked_product(kept_density, hp_product)
    pph_product = masked_product(kept_density, ph_product)
    hpp_product = masked_product(hp_product, kept_density)
    gradient = pattern * (3.0 * (hp_product + ph_product) - 2.0 * (php_product + pph_product + hpp_product))
    return (hp_product, php_product, gradient)
```

```python
import functools

import jax
import jax.numpy as jnp
from jax import lax
from jax.experimental import pallas as pl
from jax.experimental.pallas import tpu as pltpu
from jax.sharding import PartitionSpec as P

BLK = 128
VMEM_LIMIT = 40 * 1024 * 1024

highest = lax.Precision.HIGHEST


def product(leading, second):
    return jnp.dot(leading, second, precision=highest, preferred_element_type=jnp.float32)


def tile_pattern(block_mask, row_index, col_index, tile_rows, tile_cols):
    row_blocks = (row_index * tile_rows + jnp.arange(tile_rows, dtype=jnp.int32)) // BLK
    col_blocks = (col_index * tile_cols + jnp.arange(tile_cols, dtype=jnp.int32)) // BLK
    block_ids = jnp.arange(block_mask.shape[0], dtype=jnp.int32)
    row_hot = (row_blocks[:, None] == block_ids[None, :]).astype(jnp.float32)
    col_hot = (col_blocks[:, None] == block_ids[None, :]).astype(jnp.float32)
    return product(product(row_hot, block_mask.astype(jnp.float32)), col_hot.T)


def strips_body(density, hamiltonian, block_mask):
    row_index = lax.axis_index("row")
    col_index = lax.axis_index("col")
    pattern = tile_pattern(block_mask, row_index, col_index, *density.shape)
    kept_density = density * pattern
    kept_hamiltonian = hamiltonian * pattern
    density_rows = lax.all_gather(kept_density, "col", axis=1, tiled=True)
    hamiltonian_rows = lax.all_gather(kept_hamiltonian, "col", axis=1, tiled=True)
    density_strip = lax.all_gather(kept_density, "row", axis=0, tiled=True)
    hamiltonian_strip = lax.all_gather(kept_hamiltonian, "row", axis=0, tiled=True)
    hp_product = product(hamiltonian_rows, density_strip) * pattern
    ph_product = product(density_rows, hamiltonian_strip) * pattern
    hp_strip = lax.all_gather(hp_product, "row", axis=0, tiled=True)
    ph_strip = lax.all_gather(ph_product, "row", axis=0, tiled=True)
    hp_rows = lax.all_gather(hp_product, "col", axis=1, tiled=True)
    php_product = product(density_rows, hp_strip) * pattern
    pph_product = product(density_rows, ph_strip) * pattern
    hpp_product = product(hp_rows, density_strip) * pattern
    gradient = pattern * (
        3.0 * (hp_product + ph_product) - 2.0 * (php_product + pph_product + hpp_product)
    )
    return (hp_product, php_product, gradient)


ROWS, COLS = 4, 8


def swap(x, axis, mask):
    size = ROWS if axis == "row" else COLS
    return lax.ppermute(x, axis, [(i, i ^ mask) for i in range(size)])


def after(value, *others):
    return lax.optimization_barrier((value, *others))[0]


def split(x):
    high = x.astype(jnp.bfloat16)
    return high, (x - high.astype(jnp.float32)).astype(jnp.bfloat16)


def dot3(a, b):
    mul = functools.partial(jnp.dot, preferred_element_type=jnp.float32)
    return mul(a[0], b[0]) + (mul(a[0], b[1]) + mul(a[1], b[0]))


def place(r, col_block):
    band = jnp.bitwise_xor(lax.shift_right_logical(col_block, 1), r)
    start = band * (2 * BLK) + jnp.bitwise_and(col_block, 1) * BLK
    return pl.multiple_of(start, BLK)


def block_at(r, position):
    return 2 * jnp.bitwise_xor(position // 2, r) + position % 2


def pattern_of(mask_ref, row_blocks, col_blocks):
    rows = []
    for i in row_blocks:
        rows.append(
            jnp.concatenate(
                [jnp.full((BLK, BLK), mask_ref[i, j].astype(jnp.float32)) for j in col_blocks],
                axis=1,
            )
        )
    return jnp.concatenate(rows, axis=0)


def band_blocks(r, m):
    return [block_at(r, 2 * m), block_at(r, 2 * m + 1)]


def hp_kernel(mask_ref, hs, ho, p0, p1, p2, p3, hp_ref, hrow_hi, hrow_lo):
    r, c = lax.axis_index("row"), lax.axis_index("col")
    for j in range(4):
        for flip, ref in ((0, hs), (1, ho)):
            spot = place(r, jnp.bitwise_xor(c, 2 * j + flip))
            high, low = split(ref[j])
            hrow_hi[:, pl.ds(spot, BLK)] = high
            hrow_lo[:, pl.ds(spot, BLK)] = low
    total = jnp.zeros(hp_ref.shape, jnp.float32)
    for m, ref in enumerate((p0, p1, p2, p3)):
        at = pl.ds(m * 2 * BLK, 2 * BLK)
        total += dot3((hrow_hi[:, at], hrow_lo[:, at]), split(ref[...]))
    hp_ref[...] = total * pattern_of(mask_ref, band_blocks(r, 0), [c])


def z_kernel(
    mask_ref, hrow_hi, hrow_lo, a_s, a_o, b_s, b_o, h0, h1, h2, h3, hp_ref,
    z_ref, prow_hi, prow_lo, pw_hi, pw_lo,
):
    r, c = lax.axis_index("row"), lax.axis_index("col")
    band = 2 * BLK
    for j in range(4):
        for flip, first, rest in ((0, a_s, b_s), (1, a_o, b_o)):
            spot = pl.ds(place(r, jnp.bitwise_xor(c, 2 * j + flip)), BLK)
            high, low = split(first[j])
            pw_hi[0:band, spot] = high
            pw_lo[0:band, spot] = low
            high, low = split(rest[j])
            pw_hi[band:, spot] = high
            pw_lo[band:, spot] = low
    prow_hi[...] = pw_hi[0:band, :]
    prow_lo[...] = pw_lo[0:band, :]
    own = pattern_of(mask_ref, band_blocks(r, 0), [c])
    pcol = [split(a_s[0])] + [split(b_s[0, (m - 1) * band : m * band]) for m in (1, 2, 3)]
    hcol = [split(ref[...]) for ref in (h0, h1, h2, h3)]
    second = jnp.zeros((band, BLK), jnp.float32)
    ph = None
    for m in range(4):
        at = pl.ds(m * band, band)
        hp_rows = dot3((hrow_hi[...], hrow_lo[...]), (pw_hi[:, at], pw_lo[:, at]))
        hp_rows = hp_rows * pattern_of(mask_ref, band_blocks(r, 0), band_blocks(r, m))
        second += dot3(split(hp_rows), pcol[m])
        ph_rows = jnp.zeros((band, BLK), jnp.float32)
        for k in range(4):
            inner = pl.ds(k * band, band)
            ph_rows += dot3((pw_hi[at, inner], pw_lo[at, inner]), hcol[k])
        ph_rows = ph_rows * pattern_of(mask_ref, band_blocks(r, m), [c])
        if m == 0:
            ph = ph_rows
        second += dot3((pw_hi[0:band, at], pw_lo[0:band, at]), split(ph_rows))
    z_ref[...] = own * (3.0 * (hp_ref[...] + ph) - 2.0 * second)


def php_kernel(mask_ref, prow_hi, prow_lo, q0, q1, q2, q3, z_ref, php_ref, grad_ref):
    r, c = lax.axis_index("row"), lax.axis_index("col")
    total = jnp.zeros(php_ref.shape, jnp.float32)
    for m, ref in enumerate((q0, q1, q2, q3)):
        at = pl.ds(m * 2 * BLK, 2 * BLK)
        total += dot3((prow_hi[:, at], prow_lo[:, at]), split(ref[...]))
    php = total * pattern_of(mask_ref, band_blocks(r, 0), [c])
    php_ref[...] = php
    grad_ref[...] = z_ref[...] - 2.0 * php


def call(kernel, outs, scratch, flops, *args):
    smem, vmem = pl.BlockSpec(memory_space=pltpu.SMEM), pl.BlockSpec(memory_space=pltpu.VMEM)
    moved = sum(a.size * a.dtype.itemsize for a in (*args, *outs))
    return pl.pallas_call(
        kernel,
        out_shape=outs,
        in_specs=[smem] + [vmem] * (len(args) - 1),
        out_specs=tuple(vmem for _ in outs),
        scratch_shapes=scratch,
        cost_estimate=pl.CostEstimate(flops=flops, bytes_accessed=moved, transcendentals=0),
        compiler_params=pltpu.CompilerParams(vmem_limit_bytes=VMEM_LIMIT),
    )(*args)


def gather_row(x):
    return [swap(x, "row", m) for m in (1, 2, 3)]


def whole_body(density, hamiltonian, block_mask):
    r, c = lax.axis_index("row"), lax.axis_index("col")
    f32, bf16 = jnp.float32, jnp.bfloat16
    rows, cols = density.shape
    order = rows * ROWS
    tile = jax.ShapeDtypeStruct((rows, cols), f32)
    part = jax.ShapeDtypeStruct((rows, order), bf16)

    links = lax.dynamic_slice(block_mask, (2 * r, c), (2, 1)).astype(f32)
    pattern = jnp.broadcast_to(links[:, :, None], (2, BLK, cols)).reshape(rows, cols)
    p0, h0 = density * pattern, hamiltonian * pattern

    p1, p2, p3 = gather_row(p0)
    hx, hy, hd = swap(h0, "col", 2), swap(h0, "col", 4), swap(h0, "col", 6)
    hs = jnp.stack([h0, hx, hy, hd])
    ho = swap(hs, "col", 1)
    hp, hrow_hi, hrow_lo = call(
        hp_kernel, (tile, part, part), [], 6 * rows * order * cols,
        block_mask, hs, ho, p0, p1, p2, p3,
    )

    pa = after(p0, hx, hy, hd)
    ax, ay, ad = swap(pa, "col", 2), swap(pa, "col", 4), swap(pa, "col", 6)
    a_s = jnp.stack([p0, ax, ay, ad])
    a_o = swap(a_s, "col", 1)
    b = jnp.concatenate([p1, p2, p3], axis=0)
    b = after(b, ax, ay, ad)
    bx, by = swap(b, "col", 2), swap(b, "col", 4)
    half = b.shape[0] // 2
    bd_top = swap(bx[:half], "col", 4)
    bd_low = swap(by[half:], "col", 2)
    b_s = jnp.stack([b, bx, by, jnp.concatenate([bd_top, bd_low], axis=0)])
    b_o = swap(b_s, "col", 1)

    h1, h2, h3 = gather_row(after(h0, p1, p2, p3))
    q1, q2, q3 = gather_row(hp)
    z, prow_hi, prow_lo = call(
        z_kernel, (tile, part, part), [pltpu.VMEM((order, order), bf16)] * 2,
        6 * (rows * order * order + order * order * cols + 2 * rows * order * cols),
        block_mask, hrow_hi, hrow_lo, a_s, a_o, b_s, b_o, h0, h1, h2, h3, hp,
    )
    php, grad = call(
        php_kernel, (tile, tile), [], 6 * rows * order * cols,
        block_mask, prow_hi, prow_lo, hp, q1, q2, q3, z,
    )
    return hp, php, grad


def body(density, hamiltonian, block_mask, shape):
    tile_rows, tile_cols = density.shape
    if shape == (ROWS, COLS) and tile_rows == 2 * BLK and tile_cols == BLK:
        return whole_body(density, hamiltonian, block_mask)
    return strips_body(density, hamiltonian, block_mask)


def solution(mesh):
    placed = (P("row", "col"), P("row", "col"), P())
    return jax.shard_map(
        functools.partial(body, shape=(mesh.shape["row"], mesh.shape["col"])),
        mesh=mesh,
        in_specs=placed,
        out_specs=(P("row", "col"), P("row", "col"), P("row", "col")),
        check_vma=False,
    )
```

```python
import functools

import jax
import jax.numpy as jnp
from jax import lax
from jax.experimental import pallas as pl
from jax.experimental.pallas import tpu as pltpu
from jax.sharding import PartitionSpec as P

BLK = 128
VMEM_LIMIT = 40 * 1024 * 1024
AHEAD = 8

highest = lax.Precision.HIGHEST


def product(leading, second):
    return jnp.dot(leading, second, precision=highest, preferred_element_type=jnp.float32)


def tile_pattern(block_mask, row_index, col_index, tile_rows, tile_cols):
    row_blocks = (row_index * tile_rows + jnp.arange(tile_rows, dtype=jnp.int32)) // BLK
    col_blocks = (col_index * tile_cols + jnp.arange(tile_cols, dtype=jnp.int32)) // BLK
    block_ids = jnp.arange(block_mask.shape[0], dtype=jnp.int32)
    row_hot = (row_blocks[:, None] == block_ids[None, :]).astype(jnp.float32)
    col_hot = (col_blocks[:, None] == block_ids[None, :]).astype(jnp.float32)
    return product(product(row_hot, block_mask.astype(jnp.float32)), col_hot.T)


def strips_body(density, hamiltonian, block_mask):
    row_index = lax.axis_index("row")
    col_index = lax.axis_index("col")
    pattern = tile_pattern(block_mask, row_index, col_index, *density.shape)
    kept_density = density * pattern
    kept_hamiltonian = hamiltonian * pattern
    density_rows = lax.all_gather(kept_density, "col", axis=1, tiled=True)
    hamiltonian_rows = lax.all_gather(kept_hamiltonian, "col", axis=1, tiled=True)
    density_strip = lax.all_gather(kept_density, "row", axis=0, tiled=True)
    hamiltonian_strip = lax.all_gather(kept_hamiltonian, "row", axis=0, tiled=True)
    hp_product = product(hamiltonian_rows, density_strip) * pattern
    ph_product = product(density_rows, hamiltonian_strip) * pattern
    hp_strip = lax.all_gather(hp_product, "row", axis=0, tiled=True)
    ph_strip = lax.all_gather(ph_product, "row", axis=0, tiled=True)
    hp_rows = lax.all_gather(hp_product, "col", axis=1, tiled=True)
    php_product = product(density_rows, hp_strip) * pattern
    pph_product = product(density_rows, ph_strip) * pattern
    hpp_product = product(hp_rows, density_strip) * pattern
    gradient = pattern * (
        3.0 * (hp_product + ph_product) - 2.0 * (php_product + pph_product + hpp_product)
    )
    return (hp_product, php_product, gradient)


ROWS, COLS = 4, 8


def swap(x, axis, mask):
    size = ROWS if axis == "row" else COLS
    return lax.ppermute(x, axis, [(i, i ^ mask) for i in range(size)])


def after(value, *others):
    return lax.optimization_barrier((value, *others))[0]


def split(x):
    high = x.astype(jnp.bfloat16)
    return high, (x - high.astype(jnp.float32)).astype(jnp.bfloat16)


def stacked(x):
    return jnp.concatenate(split(x), axis=0)


def beside(x):
    return jnp.concatenate(split(x), axis=1)


def mul(a, b):
    return jnp.dot(a, b, preferred_element_type=jnp.float32)


def dot_parts(a, b):
    t = mul(a, b)
    m, n = t.shape[0] // 2, t.shape[1] // 2
    return (t[:m, :n] + (t[:m, n:] + t[m:, :n])) + t[m:, n:]


def dot_wide(a, b):
    t = mul(a, b[0])
    m = t.shape[0] // 2
    return t[:m] + (t[m:] + mul(a[:m], b[1]))


def dot_tall(a, b):
    t = mul(a[0], b)
    n = t.shape[1] // 2
    return t[:, :n] + (t[:, n:] + mul(a[1], b[:, :n]))


def place(r, col_block):
    band = jnp.bitwise_xor(lax.shift_right_logical(col_block, 1), r)
    start = band * (2 * BLK) + jnp.bitwise_and(col_block, 1) * BLK
    return pl.multiple_of(start, BLK)


def block_at(r, position):
    return 2 * jnp.bitwise_xor(position // 2, r) + position % 2


def pattern_of(mask_ref, row_blocks, col_blocks):
    rows = []
    for i in row_blocks:
        rows.append(
            jnp.concatenate(
                [jnp.full((BLK, BLK), mask_ref[i, j].astype(jnp.float32)) for j in col_blocks],
                axis=1,
            )
        )
    return jnp.concatenate(rows, axis=0)


def band_blocks(r, m):
    return [block_at(r, 2 * m), block_at(r, 2 * m + 1)]


BAND = 2 * BLK


def fill_rows(mask_ref, r, c, ss, so, first, out):
    for j in range(4):
        for flip, ref in ((0, ss), (1, so)):
            block = jnp.bitwise_xor(c, 2 * j + flip)
            part = ref[first + j] * pattern_of(mask_ref, band_blocks(r, 0), [block])
            out[:, pl.ds(place(r, block), BLK)] = stacked(part)


def fill_cols(mask_ref, r, c, parts, out):
    for m, part in enumerate(parts):
        kept = part * pattern_of(mask_ref, band_blocks(r, m), [c])
        out[m * BAND : (m + 1) * BAND, :] = beside(kept)


def hp_kernel(mask_ref, ss, so, p0, p1, p2, p3, hp_ref, send_ref, hrow, pcol):
    r, c = lax.axis_index("row"), lax.axis_index("col")
    fill_rows(mask_ref, r, c, ss, so, 0, hrow)
    fill_cols(mask_ref, r, c, (p0[...], p1[...], p2[...], p3[...]), pcol)
    own = pattern_of(mask_ref, band_blocks(r, 0), [c])
    tile = dot_parts(hrow[...], pcol[...]) * own
    hp_ref[...] = tile
    send_ref[0:BAND] = tile
    send_ref[BAND:] = ss[0] * own


def rows_kernel(mask_ref, ss, so, prow):
    r, c = lax.axis_index("row"), lax.axis_index("col")
    fill_rows(mask_ref, r, c, ss, so, 4, prow)


def is_middle(r):
    return jnp.logical_or(r == 1, r == 2)


def column_pairs(mask_ref, r, c, flip, first, rest):
    for j in (0, 2):
        blocks = [jnp.bitwise_xor(c, 2 * (j + i) + flip) for i in (0, 1)]
        bands = []
        for m in range(4):
            parts = []
            for i in (0, 1):
                if m == 0:
                    part = first[4 + j + i]
                else:
                    part = rest[j + i, (m - 1) * BAND : m * BAND]
                parts.append(part * pattern_of(mask_ref, band_blocks(r, m), [blocks[i]]))
            bands.append(jnp.concatenate(parts, axis=1))
        yield blocks, split(jnp.concatenate(bands, axis=0))


def rows_at(r, ref, blocks):
    return jnp.concatenate([ref[pl.ds(place(r, b), BLK), :] for b in blocks], axis=0)


def hpp_term(mask_ref, r, hrow, pcol, blocks, cols):
    hp_rows = dot_wide(hrow[...], cols)
    hp_rows = hp_rows * pattern_of(mask_ref, band_blocks(r, 0), blocks)
    return dot_parts(stacked(hp_rows), rows_at(r, pcol, blocks))


def far_rows(cols):
    return jnp.concatenate([part[BAND : 2 * BAND] for part in cols], axis=0)


def php_kernel(mask_ref, prow, q3, q1, q2, q0, php_ref, qcol, hcol):
    r, c = lax.axis_index("row"), lax.axis_index("col")
    for m, ref in enumerate((q0, q1, q2, q3)):
        qcol[m * BAND : (m + 1) * BAND, :] = beside(ref[0:BAND])
        fill = ref[BAND:] * pattern_of(mask_ref, band_blocks(r, m), [c])
        hcol[m * BAND : (m + 1) * BAND, :] = beside(fill)
    own = pattern_of(mask_ref, band_blocks(r, 0), [c])
    php_ref[...] = dot_parts(prow[...], qcol[...]) * (own * is_middle(r).astype(jnp.float32))


def own_kernel(mask_ref, hrow, hcol, pcol, ss, b_s, ph_ref, hpp_ref, far):
    r, c = lax.axis_index("row"), lax.axis_index("col")
    ph = jnp.zeros(ph_ref.shape, jnp.float32)
    hpp = jnp.zeros(hpp_ref.shape, jnp.float32)
    for n, (blocks, cols) in enumerate(column_pairs(mask_ref, r, c, 0, ss, b_s)):
        ph += dot_tall(cols, rows_at(r, hcol, blocks))
        far[:, n * BAND : (n + 1) * BAND] = far_rows(cols)
        hpp += hpp_term(mask_ref, r, hrow, pcol, blocks, cols)
    ph_ref[...] = ph
    hpp_ref[...] = hpp


def ph_kernel(mask_ref, hcol, qcol, so, b_o, part_ref, far, back_ref, tile_ref, ph2):
    r, c = lax.axis_index("row"), lax.axis_index("col")
    back_ref[...] = jnp.zeros_like(back_ref)
    tile_ref[...] = jnp.zeros_like(tile_ref)
    ph2[...] = jnp.zeros_like(ph2)

    @pl.when(is_middle(r))
    def _():
        ph = part_ref[...]
        terms = []
        for j in (0, 2):
            blocks = [jnp.bitwise_xor(c, 2 * (j + i)) for i in (0, 1)]
            terms.append((blocks, far[:, (j // 2) * BAND : (j // 2 + 1) * BAND]))
        for blocks, cols in column_pairs(mask_ref, r, c, 1, so, b_o):
            ph += dot_tall(cols, rows_at(r, hcol, blocks))
            terms.append((blocks, far_rows(cols)))
        for m in range(4):
            rows = ph[m * BAND : (m + 1) * BAND] * pattern_of(mask_ref, band_blocks(r, m), [c])
            ph2[m * BAND : (m + 1) * BAND, :] = beside(rows)
            if m == 0:
                tile_ref[...] = rows
            if m == 1:
                beyond = rows
        pph = jnp.zeros(tile_ref.shape, jnp.float32)
        php = jnp.zeros(tile_ref.shape, jnp.float32)
        for blocks, left in terms:
            pph += dot_parts(left, rows_at(r, ph2, blocks))
            php += dot_parts(left, rows_at(r, qcol, blocks))
        there = pattern_of(mask_ref, band_blocks(r, 1), [c])
        back_ref[0:BAND] = there * (3.0 * beyond - 2.0 * (pph + php))
        back_ref[BAND:] = there * php


def last_kernel(
    mask_ref, prow, hrow, pcol, so, b_o, ph2, hp_ref, ph_ref, hpp_ref, php_ref, grad_ref
):
    r, c = lax.axis_index("row"), lax.axis_index("col")
    second = hpp_ref[...] + dot_parts(prow[...], ph2[...])
    for blocks, cols in column_pairs(mask_ref, r, c, 1, so, b_o):
        second += hpp_term(mask_ref, r, hrow, pcol, blocks, cols)
    own = pattern_of(mask_ref, band_blocks(r, 0), [c])
    grad_ref[...] = 3.0 * (hp_ref[...] + ph_ref[...]) - 2.0 * (php_ref[...] + own * second)


def call(kernel, outs, scratch, flops, *args):
    smem, vmem = pl.BlockSpec(memory_space=pltpu.SMEM), pl.BlockSpec(memory_space=pltpu.VMEM)
    moved = sum(a.size * a.dtype.itemsize for a in (*args, *outs))
    return pl.pallas_call(
        kernel,
        out_shape=outs,
        in_specs=[smem] + [vmem] * (len(args) - 1),
        out_specs=tuple(vmem for _ in outs),
        scratch_shapes=scratch,
        cost_estimate=pl.CostEstimate(flops=flops, bytes_accessed=moved, transcendentals=0),
        compiler_params=pltpu.CompilerParams(vmem_limit_bytes=VMEM_LIMIT),
    )(*args)


def to_middle(x):
    routes = [
        [(0, 1), (3, 2), (1, 0), (2, 3)],
        [(0, 2), (3, 1), (1, 0), (2, 3)],
        [(1, 2), (2, 1), (0, 0), (3, 3)],
    ]
    return [lax.ppermute(x, "row", pairs) for pairs in routes]


def whole_body(density, hamiltonian, block_mask):
    f32, bf16 = jnp.float32, jnp.bfloat16
    rows, cols = density.shape
    order = rows * ROWS

    def shape(a, b, dtype=bf16):
        return jax.ShapeDtypeStruct((a, b), dtype)

    tile, strip = shape(rows, cols, f32), shape(order, cols, f32)
    rows2, cols2 = shape(2 * rows, order), shape(order, 2 * cols)
    weight = 6 * rows * order * order
    p0, h0 = density, hamiltonian
    hx, py = swap(h0, "col", 2), swap(p0, "col", 4)
    both = lax.optimization_barrier(jnp.concatenate([p0, h0], axis=0))
    p0, h0 = both[:rows], both[rows:]
    p1, p2, p3 = [swap(p0, "row", m) for m in (1, 2, 3)]
    hy = swap(jnp.concatenate([h0, hx], axis=0), "col", 4)
    px = swap(jnp.concatenate([p0, py], axis=0), "col", 2)
    p1, p2, p3, hy, px = lax.optimization_barrier((p1, p2, p3, hy, px))
    ss = jnp.stack([h0, hx, hy[:rows], hy[rows:], p0, px[:rows], py, px[rows:]])
    so = swap(ss, "col", 1)

    b = jnp.concatenate([p1, p2, p3], axis=0)
    half = b.shape[0] // 2
    upper, lower = b[:half], b[half:]
    ux, ly = swap(upper, "col", 2), swap(lower, "col", 4)

    hp, send, hrow, pcol = call(
        hp_kernel, (tile, shape(2 * rows, cols, f32), rows2, cols2), [], weight,
        block_mask, ss, so, p0, p1, p2, p3,
    )
    q1, q2, q3 = to_middle(send)
    uy = swap(jnp.concatenate([upper, ux], axis=0), "col", 4)
    lx = swap(jnp.concatenate([lower, ly], axis=0), "col", 2)
    (prow,) = call(rows_kernel, (rows2,), [], weight, block_mask, ss, so)
    php, qcol, hcol = call(
        php_kernel, (tile, cols2, cols2), [], AHEAD * weight, block_mask, prow, q3, q1, q2, send
    )
    uy, lx, php = lax.optimization_barrier((uy, lx, php))
    b_s = jnp.stack(
        [
            jnp.concatenate(pair, axis=0)
            for pair in ((upper, lower), (ux, lx[:half]), (uy[:half], ly), (uy[half:], lx[half:]))
        ]
    )
    b_o = swap(b_s, "col", 1)

    part, hpp, far = call(
        own_kernel, (strip, tile, shape(2 * rows, order // 2)), [], weight,
        block_mask, hrow, hcol, pcol, ss, b_s,
    )
    back, ph, ph2 = call(
        ph_kernel, (shape(2 * rows, cols, f32), tile, cols2), [], weight,
        block_mask, hcol, qcol, so, b_o, part, far,
    )
    got = lax.ppermute(back, "row", [(1, 0), (2, 3)])
    (grad,) = call(
        last_kernel, (tile,), [], weight,
        block_mask, prow, hrow, pcol, so, b_o, ph2, hp, ph, hpp, php,
    )
    return hp, php + got[rows:], grad + got[:rows]


def body(density, hamiltonian, block_mask, shape):
    tile_rows, tile_cols = density.shape
    if shape == (ROWS, COLS) and tile_rows == 2 * BLK and tile_cols == BLK:
        return whole_body(density, hamiltonian, block_mask)
    return strips_body(density, hamiltonian, block_mask)


def solution(mesh):
    placed = (P("row", "col"), P("row", "col"), P())
    return jax.shard_map(
        functools.partial(body, shape=(mesh.shape["row"], mesh.shape["col"])),
        mesh=mesh,
        in_specs=placed,
        out_specs=(P("row", "col"), P("row", "col"), P("row", "col")),
        check_vma=False,
    )
```

```python
import functools

import jax
import jax.numpy as jnp
from jax import lax
from jax.experimental import pallas as pl
from jax.experimental.pallas import tpu as pltpu
from jax.sharding import PartitionSpec as P

BLK = 128
VMEM_LIMIT = 40 * 1024 * 1024
AHEAD = 8

highest = lax.Precision.HIGHEST


def product(leading, second):
    return jnp.dot(leading, second, precision=highest, preferred_element_type=jnp.float32)


def tile_pattern(block_mask, row_index, col_index, tile_rows, tile_cols):
    row_blocks = (row_index * tile_rows + jnp.arange(tile_rows, dtype=jnp.int32)) // BLK
    col_blocks = (col_index * tile_cols + jnp.arange(tile_cols, dtype=jnp.int32)) // BLK
    block_ids = jnp.arange(block_mask.shape[0], dtype=jnp.int32)
    row_hot = (row_blocks[:, None] == block_ids[None, :]).astype(jnp.float32)
    col_hot = (col_blocks[:, None] == block_ids[None, :]).astype(jnp.float32)
    return product(product(row_hot, block_mask.astype(jnp.float32)), col_hot.T)


def strips_body(density, hamiltonian, block_mask):
    row_index = lax.axis_index("row")
    col_index = lax.axis_index("col")
    pattern = tile_pattern(block_mask, row_index, col_index, *density.shape)
    kept_density = density * pattern
    kept_hamiltonian = hamiltonian * pattern
    density_rows = lax.all_gather(kept_density, "col", axis=1, tiled=True)
    hamiltonian_rows = lax.all_gather(kept_hamiltonian, "col", axis=1, tiled=True)
    density_strip = lax.all_gather(kept_density, "row", axis=0, tiled=True)
    hamiltonian_strip = lax.all_gather(kept_hamiltonian, "row", axis=0, tiled=True)
    hp_product = product(hamiltonian_rows, density_strip) * pattern
    ph_product = product(density_rows, hamiltonian_strip) * pattern
    hp_strip = lax.all_gather(hp_product, "row", axis=0, tiled=True)
    ph_strip = lax.all_gather(ph_product, "row", axis=0, tiled=True)
    hp_rows = lax.all_gather(hp_product, "col", axis=1, tiled=True)
    php_product = product(density_rows, hp_strip) * pattern
    pph_product = product(density_rows, ph_strip) * pattern
    hpp_product = product(hp_rows, density_strip) * pattern
    gradient = pattern * (
        3.0 * (hp_product + ph_product) - 2.0 * (php_product + pph_product + hpp_product)
    )
    return (hp_product, php_product, gradient)


ROWS, COLS = 4, 8


def swap(x, axis, mask):
    size = ROWS if axis == "row" else COLS
    return lax.ppermute(x, axis, [(i, i ^ mask) for i in range(size)])


def after(value, *others):
    return lax.optimization_barrier((value, *others))[0]


def split(x):
    high = x.astype(jnp.bfloat16)
    return high, (x - high.astype(jnp.float32)).astype(jnp.bfloat16)


def stacked(x):
    return jnp.concatenate(split(x), axis=0)


def beside(x):
    return jnp.concatenate(split(x), axis=1)


def mul(a, b):
    return jnp.dot(a, b, preferred_element_type=jnp.float32)


def dot_parts(a, b):
    t = mul(a, b)
    m, n = t.shape[0] // 2, t.shape[1] // 2
    return (t[:m, :n] + (t[:m, n:] + t[m:, :n])) + t[m:, n:]


def dot_wide(a, b):
    t = mul(a, b[0])
    m = t.shape[0] // 2
    return t[:m] + (t[m:] + mul(a[:m], b[1]))


def dot_tall(a, b):
    t = mul(a[0], b)
    n = t.shape[1] // 2
    return t[:, :n] + (t[:, n:] + mul(a[1], b[:, :n]))


def place(r, col_block):
    band = jnp.bitwise_xor(lax.shift_right_logical(col_block, 1), r)
    start = band * (2 * BLK) + jnp.bitwise_and(col_block, 1) * BLK
    return pl.multiple_of(start, BLK)


def block_at(r, position):
    return 2 * jnp.bitwise_xor(position // 2, r) + position % 2


def pattern_of(mask_ref, row_blocks, col_blocks):
    rows = []
    for i in row_blocks:
        rows.append(
            jnp.concatenate(
                [jnp.full((BLK, BLK), mask_ref[i, j].astype(jnp.float32)) for j in col_blocks],
                axis=1,
            )
        )
    return jnp.concatenate(rows, axis=0)


def band_blocks(r, m):
    return [block_at(r, 2 * m), block_at(r, 2 * m + 1)]


BAND = 2 * BLK


def fill_rows(mask_ref, r, c, ss, so, first, out):
    for j in range(4):
        for flip, ref in ((0, ss), (1, so)):
            block = jnp.bitwise_xor(c, 2 * j + flip)
            part = ref[first + j] * pattern_of(mask_ref, band_blocks(r, 0), [block])
            out[:, pl.ds(place(r, block), BLK)] = stacked(part)


def fill_cols(mask_ref, r, c, parts, out):
    for m, part in enumerate(parts):
        kept = part * pattern_of(mask_ref, band_blocks(r, m), [c])
        out[m * BAND : (m + 1) * BAND, :] = beside(kept)


def left_pair(mask_ref, r, blocks, first, at):
    parts = [
        first[at + i] * pattern_of(mask_ref, band_blocks(r, 0), [blocks[i]]) for i in (0, 1)
    ]
    return stacked(jnp.concatenate(parts, axis=1))


def pairs(c, flip):
    for j in (0, 2):
        yield j, [jnp.bitwise_xor(c, 2 * (j + i) + flip) for i in (0, 1)]


def start_kernel(mask_ref, p0, p1, p2, p3, ss, part_ref, pcol):
    r, c = lax.axis_index("row"), lax.axis_index("col")
    fill_cols(mask_ref, r, c, (p0[...], p1[...], p2[...], p3[...]), pcol)
    total = jnp.zeros(part_ref.shape, jnp.float32)
    for j, blocks in pairs(c, 0):
        total += dot_parts(left_pair(mask_ref, r, blocks, ss, j), rows_at(r, pcol, blocks))
    part_ref[...] = total


def hp_kernel(mask_ref, part_ref, pcol, ss, so, send_ref, mark_ref):
    r, c = lax.axis_index("row"), lax.axis_index("col")
    total = part_ref[...]
    for j, blocks in pairs(c, 1):
        total += dot_parts(left_pair(mask_ref, r, blocks, so, j), rows_at(r, pcol, blocks))
    own = pattern_of(mask_ref, band_blocks(r, 0), [c])
    send_ref[0:BAND] = total * own
    send_ref[BAND:] = ss[0] * own
    mark_ref[...] = jnp.zeros_like(mark_ref)


def rows_kernel(mask_ref, ss, so, send_ref, mark_ref, hrow, prow, hp_ref):
    r, c = lax.axis_index("row"), lax.axis_index("col")
    hp_ref[...] = send_ref[0:BAND]
    fill_rows(mask_ref, r, c, ss, so, 0, hrow)
    fill_rows(mask_ref, r, c, ss, so, 4, prow)


def is_middle(r):
    return jnp.logical_or(r == 1, r == 2)


def tile_of(mask_ref, r, block, j, m, first, rest):
    part = first[4 + j] if m == 0 else rest[j % 2, (m - 1) * BAND : m * BAND]
    return part * pattern_of(mask_ref, band_blocks(r, m), [block])


def meets(mask_ref, r, m, block):
    return sum(mask_ref[i, block] for i in band_blocks(r, m)) != 0


def block_of(c, j, flip):
    return jnp.bitwise_xor(c, 2 * j + flip)


def rows_at(r, ref, blocks):
    return jnp.concatenate([ref[pl.ds(place(r, b), BLK), :] for b in blocks], axis=0)


def php_kernel(mask_ref, prow, q3, q1, q2, q0, php_ref, hcol, across_ref, qcol):
    r, c = lax.axis_index("row"), lax.axis_index("col")
    for m, ref in enumerate((q0, q1, q2, q3)):
        qcol[m * BAND : (m + 1) * BAND, :] = beside(ref[0:BAND])
        fill = ref[BAND:] * pattern_of(mask_ref, band_blocks(r, m), [c])
        hcol[m * BAND : (m + 1) * BAND, :] = beside(fill)
    own = pattern_of(mask_ref, band_blocks(r, 0), [c])
    php_ref[...] = dot_parts(prow[...], qcol[...]) * own
    across_ref[0:BAND] = q3[0:BAND]
    across_ref[BAND:] = q2[0:BAND]


def add_ph(mask_ref, r, c, flip, j, first, rest, hcol, ph_ref, far, slot):
    block = block_of(c, j, flip)

    @pl.when(mask_ref[block, c] != 0)
    def _():
        right = rows_at(r, hcol, [block])
        for m in range(4):
            at = pl.ds(m * BAND, BAND)
            if m == 1:
                left = stacked(tile_of(mask_ref, r, block, j, m, first, rest))
                far[:, slot * BLK : (slot + 1) * BLK] = left
                ph_ref[at, :] += dot_parts(left, right)
                continue

            @pl.when(jnp.logical_and(meets(mask_ref, r, m, block), meets(mask_ref, r, m, c)))
            def _(m=m, at=at):
                left = stacked(tile_of(mask_ref, r, block, j, m, first, rest))
                ph_ref[at, :] += dot_parts(left, right)


def own_kernel(mask_ref, hcol, ss, lo, hi, ph_ref, far):
    r, c = lax.axis_index("row"), lax.axis_index("col")

    @pl.when(is_middle(r))
    def _():
        ph_ref[...] = jnp.zeros_like(ph_ref)
        for j in range(4):
            add_ph(mask_ref, r, c, 0, j, ss, (lo, hi)[j // 2], hcol, ph_ref, far, j)


def other_kernel(mask_ref, hcol, so, hi, part_ref, ph_ref, far):
    r, c = lax.axis_index("row"), lax.axis_index("col")

    @pl.when(is_middle(r))
    def _():
        ph_ref[...] = part_ref[...]
        for j in (2, 3):
            add_ph(mask_ref, r, c, 1, j, so, hi, hcol, ph_ref, far, j - 2)


def ph_kernel(
    mask_ref, hcol, so, lo, part_ref, far_own, far_hi, back_ref, tile_ref, ph2, ph_ref, far_lo
):
    r, c = lax.axis_index("row"), lax.axis_index("col")
    back_ref[...] = jnp.zeros_like(back_ref)
    tile_ref[...] = jnp.zeros_like(tile_ref)
    ph2[...] = jnp.zeros_like(ph2)

    @pl.when(is_middle(r))
    def _():
        ph_ref[...] = part_ref[...]
        for j in (0, 1):
            add_ph(mask_ref, r, c, 1, j, so, lo, hcol, ph_ref, far_lo, j)
        for m in range(4):
            at = pl.ds(m * BAND, BAND)
            rows = ph_ref[at, :] * pattern_of(mask_ref, band_blocks(r, m), [c])
            ph2[at, :] = beside(rows)
            if m == 0:
                tile_ref[...] = rows
            if m == 1:
                back_ref[...] = 3.0 * rows
        there = pattern_of(mask_ref, band_blocks(r, 1), [c])
        for flip, far, j, slot in (
            *((0, far_own, j, j) for j in range(4)),
            *((1, far_lo, j, j) for j in (0, 1)),
            *((1, far_hi, j, j - 2) for j in (2, 3)),
        ):
            block = block_of(c, j, flip)

            @pl.when(mask_ref[block, c] != 0)
            def _(far=far, slot=slot, block=block):
                left = far[:, slot * BLK : (slot + 1) * BLK]
                back_ref[...] -= 2.0 * there * dot_parts(left, rows_at(r, ph2, [block]))


def last_kernel(
    mask_ref, prow, hrow, pcol, ss, so, s_lo, s_hi, o_lo, o_hi, ph2, send_ref, q1, q23,
    ph_ref, part_ref, php_ref, grad_ref, qcol, acc, row_acc,
):
    r, c = lax.axis_index("row"), lax.axis_index("col")
    own = pattern_of(mask_ref, band_blocks(r, 0), [c])
    hp = send_ref[0:BAND]

    @pl.when(is_middle(r))
    def _():
        php_ref[...] = part_ref[...]
        acc[...] = dot_parts(prow[...], ph2[...])

    @pl.when(jnp.logical_not(is_middle(r)))
    def _():
        for m, part in enumerate((hp, q1[0:BAND], q23[0:BAND], q23[BAND:])):
            qcol[m * BAND : (m + 1) * BAND, :] = beside(part)
        php_ref[...] = dot_parts(prow[...], qcol[...]) * own
        acc[...] = jnp.zeros_like(acc)

    acc[...] += dot_parts(stacked(hp), rows_at(r, pcol, [c]))
    for flip, first, rests in ((0, ss, (s_lo, s_hi)), (1, so, (o_lo, o_hi))):
        for j in range(1 - flip, 4):
            block = block_of(c, j, flip)

            @pl.when(mask_ref[block, c] != 0)
            def _(first=first, rest=rests[j // 2], j=j, block=block):
                row_acc[...] = jnp.zeros_like(row_acc)
                for m in range(4):

                    @pl.when(meets(mask_ref, r, m, block))
                    def _(m=m):
                        right = beside(tile_of(mask_ref, r, block, j, m, first, rest))
                        row_acc[...] += dot_parts(hrow[:, m * BAND : (m + 1) * BAND], right)

                rows = row_acc[...] * pattern_of(mask_ref, band_blocks(r, 0), [block])
                acc[...] += dot_parts(stacked(rows), rows_at(r, pcol, [block]))

    grad_ref[...] = 3.0 * (hp + ph_ref[...]) - 2.0 * (php_ref[...] + own * acc[...])


def call(kernel, outs, scratch, flops, *args):
    smem, vmem = pl.BlockSpec(memory_space=pltpu.SMEM), pl.BlockSpec(memory_space=pltpu.VMEM)
    moved = sum(a.size * a.dtype.itemsize for a in (*args, *outs))
    return pl.pallas_call(
        kernel,
        out_shape=outs,
        in_specs=[smem] + [vmem] * (len(args) - 1),
        out_specs=tuple(vmem for _ in outs),
        scratch_shapes=scratch,
        cost_estimate=pl.CostEstimate(flops=flops, bytes_accessed=moved, transcendentals=0),
        compiler_params=pltpu.CompilerParams(vmem_limit_bytes=VMEM_LIMIT),
    )(*args)


def to_middle(x):
    routes = [
        [(0, 1), (3, 2), (1, 0), (2, 3)],
        [(0, 2), (3, 1), (1, 0), (2, 3)],
        [(1, 2), (2, 1), (0, 0), (3, 3)],
    ]
    return [lax.ppermute(x, "row", pairs) for pairs in routes]


def whole_body(density, hamiltonian, block_mask):
    f32, bf16 = jnp.float32, jnp.bfloat16
    rows, cols = density.shape
    order = rows * ROWS

    def shape(a, b, dtype=bf16):
        return jax.ShapeDtypeStruct((a, b), dtype)

    tile, strip = shape(rows, cols, f32), shape(order, cols, f32)
    rows2, cols2 = shape(2 * rows, order), shape(order, 2 * cols)
    weight = 6 * rows * order * order
    p0, h0 = density, hamiltonian
    hx, py = swap(h0, "col", 2), swap(p0, "col", 4)
    p3 = swap(p0, "row", 3)
    both = lax.optimization_barrier(jnp.concatenate([p0, h0], axis=0))
    p0, h0 = both[:rows], both[rows:]
    p1, p2 = swap(p0, "row", 1), swap(p0, "row", 2)
    hy = swap(jnp.concatenate([h0, hx], axis=0), "col", 4)
    px = swap(jnp.concatenate([p0, py], axis=0), "col", 2)
    p1, p2, p3, hy, px = lax.optimization_barrier((p1, p2, p3, hy, px))
    ss = jnp.stack([h0, hx, hy[:rows], hy[rows:], p0, px[:rows], py, px[rows:]])
    so = swap(ss, "col", 1)

    b = jnp.concatenate([p1, p2, p3], axis=0)
    half = b.shape[0] // 2
    upper, lower = b[:half], b[half:]
    ux, ly = swap(upper, "col", 2), swap(lower, "col", 4)

    part, pcol = call(start_kernel, (tile, cols2), [], weight, block_mask, p0, p1, p2, p3, ss)
    send, mark = call(
        hp_kernel, (shape(2 * rows, cols, f32), shape(8, cols, f32)), [], weight,
        block_mask, part, pcol, ss, so,
    )
    ux, ly, mark = lax.optimization_barrier((ux, ly, mark))
    q1, q2, q3 = to_middle(send)
    uy = swap(jnp.concatenate([upper, ux], axis=0), "col", 4)
    lx = swap(jnp.concatenate([lower, ly], axis=0), "col", 2)
    hrow, prow, hp = call(
        rows_kernel, (rows2, rows2, tile), [], weight, block_mask, ss, so, send, mark
    )
    php, hcol, across = call(
        php_kernel, (tile, cols2, shape(2 * rows, cols, f32)),
        [pltpu.VMEM((order, 2 * cols), bf16)], AHEAD * weight,
        block_mask, prow, q3, q1, q2, send,
    )
    q23 = swap(across, "row", 1)
    uy, lx, php = lax.optimization_barrier((uy, lx, php))
    s_lo = jnp.stack([b, jnp.concatenate([ux, lx[:half]], axis=0)])
    s_hi = jnp.stack([jnp.concatenate(pair, axis=0) for pair in ((uy[:half], ly), (uy[half:], lx[half:]))])
    o_lo, o_hi = swap(s_lo, "col", 1), swap(s_hi, "col", 1)

    half_far, quarter_far = shape(2 * rows, order // 2), shape(2 * rows, order // 4)
    strip_acc = pltpu.VMEM((order, cols), f32)
    part, far_own = call(
        own_kernel, (strip, half_far), [], AHEAD * weight, block_mask, hcol, ss, s_lo, s_hi
    )
    part, far_hi = call(
        other_kernel, (strip, quarter_far), [], weight, block_mask, hcol, so, o_hi, part
    )
    back, ph, ph2 = call(
        ph_kernel, (tile, tile, cols2), [strip_acc, pltpu.VMEM((2 * rows, order // 4), bf16)],
        weight, block_mask, hcol, so, o_lo, part, far_own, far_hi,
    )
    got = lax.ppermute(back, "row", [(1, 0), (2, 3)])
    php, grad = call(
        last_kernel, (tile, tile),
        [pltpu.VMEM((order, 2 * cols), bf16)] + [pltpu.VMEM((rows, cols), f32)] * 2, weight,
        block_mask, prow, hrow, pcol, ss, so, s_lo, s_hi, o_lo, o_hi, ph2, send, q1, q23, ph, php,
    )
    return hp, php, grad + got


def body(density, hamiltonian, block_mask, shape):
    tile_rows, tile_cols = density.shape
    if shape == (ROWS, COLS) and tile_rows == 2 * BLK and tile_cols == BLK:
        return whole_body(density, hamiltonian, block_mask)
    return strips_body(density, hamiltonian, block_mask)


def solution(mesh):
    placed = (P("row", "col"), P("row", "col"), P())
    return jax.shard_map(
        functools.partial(body, shape=(mesh.shape["row"], mesh.shape["col"])),
        mesh=mesh,
        in_specs=placed,
        out_specs=(P("row", "col"), P("row", "col"), P("row", "col")),
        check_vma=False,
    )
```

```python
import functools

import jax
import jax.numpy as jnp
from jax import lax
from jax.experimental import pallas as pl
from jax.experimental.pallas import tpu as pltpu
from jax.sharding import PartitionSpec as P

BLK = 128
VMEM_LIMIT = 40 * 1024 * 1024
AHEAD = 8

highest = lax.Precision.HIGHEST


def product(leading, second):
    return jnp.dot(leading, second, precision=highest, preferred_element_type=jnp.float32)


def tile_pattern(block_mask, row_index, col_index, tile_rows, tile_cols):
    row_blocks = (row_index * tile_rows + jnp.arange(tile_rows, dtype=jnp.int32)) // BLK
    col_blocks = (col_index * tile_cols + jnp.arange(tile_cols, dtype=jnp.int32)) // BLK
    block_ids = jnp.arange(block_mask.shape[0], dtype=jnp.int32)
    row_hot = (row_blocks[:, None] == block_ids[None, :]).astype(jnp.float32)
    col_hot = (col_blocks[:, None] == block_ids[None, :]).astype(jnp.float32)
    return product(product(row_hot, block_mask.astype(jnp.float32)), col_hot.T)


def strips_body(density, hamiltonian, block_mask):
    row_index = lax.axis_index("row")
    col_index = lax.axis_index("col")
    pattern = tile_pattern(block_mask, row_index, col_index, *density.shape)
    kept_density = density * pattern
    kept_hamiltonian = hamiltonian * pattern
    density_rows = lax.all_gather(kept_density, "col", axis=1, tiled=True)
    hamiltonian_rows = lax.all_gather(kept_hamiltonian, "col", axis=1, tiled=True)
    density_strip = lax.all_gather(kept_density, "row", axis=0, tiled=True)
    hamiltonian_strip = lax.all_gather(kept_hamiltonian, "row", axis=0, tiled=True)
    hp_product = product(hamiltonian_rows, density_strip) * pattern
    ph_product = product(density_rows, hamiltonian_strip) * pattern
    hp_strip = lax.all_gather(hp_product, "row", axis=0, tiled=True)
    ph_strip = lax.all_gather(ph_product, "row", axis=0, tiled=True)
    hp_rows = lax.all_gather(hp_product, "col", axis=1, tiled=True)
    php_product = product(density_rows, hp_strip) * pattern
    pph_product = product(density_rows, ph_strip) * pattern
    hpp_product = product(hp_rows, density_strip) * pattern
    gradient = pattern * (
        3.0 * (hp_product + ph_product) - 2.0 * (php_product + pph_product + hpp_product)
    )
    return (hp_product, php_product, gradient)


ROWS, COLS = 4, 8


def swap(x, axis, mask):
    size = ROWS if axis == "row" else COLS
    return lax.ppermute(x, axis, [(i, i ^ mask) for i in range(size)])


def after(value, *others):
    return lax.optimization_barrier((value, *others))[0]


def split(x):
    high = x.astype(jnp.bfloat16)
    return high, (x - high.astype(jnp.float32)).astype(jnp.bfloat16)


def stacked(x):
    return jnp.concatenate(split(x), axis=0)


def beside(x):
    return jnp.concatenate(split(x), axis=1)


def mul(a, b):
    return jnp.dot(a, b, preferred_element_type=jnp.float32)


def dot_parts(a, b):
    t = mul(a, b)
    m, n = t.shape[0] // 2, t.shape[1] // 2
    return (t[:m, :n] + (t[:m, n:] + t[m:, :n])) + t[m:, n:]


def dot_wide(a, b):
    t = mul(a, b[0])
    m = t.shape[0] // 2
    return t[:m] + (t[m:] + mul(a[:m], b[1]))


def dot_tall(a, b):
    t = mul(a[0], b)
    n = t.shape[1] // 2
    return t[:, :n] + (t[:, n:] + mul(a[1], b[:, :n]))


def place(r, col_block):
    band = jnp.bitwise_xor(lax.shift_right_logical(col_block, 1), r)
    start = band * (2 * BLK) + jnp.bitwise_and(col_block, 1) * BLK
    return pl.multiple_of(start, BLK)


def block_at(r, position):
    return 2 * jnp.bitwise_xor(position // 2, r) + position % 2


def pattern_of(mask_ref, row_blocks, col_blocks):
    rows = []
    for i in row_blocks:
        rows.append(
            jnp.concatenate(
                [jnp.full((BLK, BLK), mask_ref[i, j].astype(jnp.float32)) for j in col_blocks],
                axis=1,
            )
        )
    return jnp.concatenate(rows, axis=0)


def band_blocks(r, m):
    return [block_at(r, 2 * m), block_at(r, 2 * m + 1)]


BAND = 2 * BLK


def fill_rows(mask_ref, r, c, ss, so, first, out):
    for j in range(4):
        for flip, ref in ((0, ss), (1, so)):
            block = jnp.bitwise_xor(c, 2 * j + flip)
            part = ref[first + j] * pattern_of(mask_ref, band_blocks(r, 0), [block])
            out[:, pl.ds(place(r, block), BLK)] = stacked(part)


def fill_cols(mask_ref, r, c, parts, out):
    for m, part in enumerate(parts):
        kept = part * pattern_of(mask_ref, band_blocks(r, m), [c])
        out[m * BAND : (m + 1) * BAND, :] = beside(kept)


def left_pair(mask_ref, r, blocks, first, at):
    parts = [
        first[at + i] * pattern_of(mask_ref, band_blocks(r, 0), [blocks[i]]) for i in (0, 1)
    ]
    return stacked(jnp.concatenate(parts, axis=1))


def pairs(c, flip):
    for j in (0, 2):
        yield j, [jnp.bitwise_xor(c, 2 * (j + i) + flip) for i in (0, 1)]


def start_kernel(mask_ref, p0, p1, p2, p3, ss, part_ref, pcol):
    r, c = lax.axis_index("row"), lax.axis_index("col")
    fill_cols(mask_ref, r, c, (p0[...], p1[...], p2[...], p3[...]), pcol)
    total = jnp.zeros(part_ref.shape, jnp.float32)
    for j, blocks in pairs(c, 0):
        total += dot_parts(left_pair(mask_ref, r, blocks, ss, j), rows_at(r, pcol, blocks))
    part_ref[...] = total


def hp_kernel(mask_ref, part_ref, pcol, ss, so, send_ref, mark_ref):
    r, c = lax.axis_index("row"), lax.axis_index("col")
    total = part_ref[...]
    for j, blocks in pairs(c, 1):
        total += dot_parts(left_pair(mask_ref, r, blocks, so, j), rows_at(r, pcol, blocks))
    own = pattern_of(mask_ref, band_blocks(r, 0), [c])
    send_ref[0:BAND] = total * own
    send_ref[BAND:] = ss[0] * own
    mark_ref[...] = jnp.zeros_like(mark_ref)


def rows_kernel(mask_ref, ss, so, send_ref, mark_ref, hrow, prow, hp_ref):
    r, c = lax.axis_index("row"), lax.axis_index("col")
    hp_ref[...] = send_ref[0:BAND]
    fill_rows(mask_ref, r, c, ss, so, 0, hrow)
    fill_rows(mask_ref, r, c, ss, so, 4, prow)


def is_middle(r):
    return jnp.logical_or(r == 1, r == 2)


def column_pair(mask_ref, r, blocks, j, first, rest):
    bands = []
    for m in range(4):
        parts = []
        for i in (0, 1):
            part = first[4 + j + i] if m == 0 else rest[i, (m - 1) * BAND : m * BAND]
            parts.append(part * pattern_of(mask_ref, band_blocks(r, m), [blocks[i]]))
        bands.append(jnp.concatenate(parts, axis=1))
    return split(jnp.concatenate(bands, axis=0))


def rows_at(r, ref, blocks):
    return jnp.concatenate([ref[pl.ds(place(r, b), BLK), :] for b in blocks], axis=0)


def far_rows(cols):
    return jnp.concatenate([part[BAND : 2 * BAND] for part in cols], axis=0)


def h_kernel(mask_ref, q3, q1, q2, q0, hcol, across_ref):
    r, c = lax.axis_index("row"), lax.axis_index("col")
    fill_cols(mask_ref, r, c, [ref[BAND:] for ref in (q0, q1, q2, q3)], hcol)
    across_ref[0:BAND] = q3[0:BAND]
    across_ref[BAND:] = q2[0:BAND]


def any_live(mask_ref, blocks, c):
    return sum(mask_ref[b, c] for b in blocks) != 0


def add_ph(mask_ref, r, c, pair, first, rest, hcol, ph_ref, far):
    j, blocks = pair

    @pl.when(any_live(mask_ref, blocks, c))
    def _():
        cols = column_pair(mask_ref, r, blocks, j, first, rest)
        ph_ref[...] += dot_tall(cols, rows_at(r, hcol, blocks))
        far[...] = far_rows(cols)


def php_of(mask_ref, r, c, parts, prow, qcol):
    for m, part in enumerate(parts):
        qcol[m * BAND : (m + 1) * BAND, :] = beside(part)
    own = pattern_of(mask_ref, band_blocks(r, 0), [c])
    return dot_parts(prow[...], qcol[...]) * own


def own_kernel(
    mask_ref, hcol, ss, lo, hi, prow, q0, q1, q2, q3, ph_ref, far_lo, far_hi, php_ref, qcol
):
    r, c = lax.axis_index("row"), lax.axis_index("col")

    @pl.when(is_middle(r))
    def _():
        parts = [ref[0:BAND] for ref in (q0, q1, q2, q3)]
        php_ref[...] = php_of(mask_ref, r, c, parts, prow, qcol)
        ph_ref[...] = jnp.zeros_like(ph_ref)
        for pair, rest, far in zip(pairs(c, 0), (lo, hi), (far_lo, far_hi)):
            add_ph(mask_ref, r, c, pair, ss, rest, hcol, ph_ref, far)


def other_kernel(mask_ref, hcol, so, hi, part_ref, ph_ref, far):
    r, c = lax.axis_index("row"), lax.axis_index("col")

    @pl.when(is_middle(r))
    def _():
        ph_ref[...] = part_ref[...]
        _, pair = pairs(c, 1)
        add_ph(mask_ref, r, c, pair, so, hi, hcol, ph_ref, far)


def ph_kernel(
    mask_ref, hcol, so, lo, part_ref, own_lo, own_hi, other_hi, back_ref, tile_ref, ph2,
    ph_ref, other_lo,
):
    r, c = lax.axis_index("row"), lax.axis_index("col")
    back_ref[...] = jnp.zeros_like(back_ref)
    tile_ref[...] = jnp.zeros_like(tile_ref)
    ph2[...] = jnp.zeros_like(ph2)

    @pl.when(is_middle(r))
    def _():
        ph_ref[...] = part_ref[...]
        add_ph(mask_ref, r, c, next(pairs(c, 1)), so, lo, hcol, ph_ref, other_lo)
        for m in range(4):
            at = pl.ds(m * BAND, BAND)
            rows = ph_ref[at, :] * pattern_of(mask_ref, band_blocks(r, m), [c])
            ph2[at, :] = beside(rows)
            if m == 0:
                tile_ref[...] = rows
            if m == 1:
                back_ref[...] = 3.0 * rows
        there = pattern_of(mask_ref, band_blocks(r, 1), [c])
        fars = ((0, (own_lo, own_hi)), (1, (other_lo, other_hi)))
        for flip, parts in fars:
            for (_, blocks), far in zip(pairs(c, flip), parts):

                @pl.when(any_live(mask_ref, blocks, c))
                def _(blocks=blocks, far=far):
                    term = dot_parts(far[...], rows_at(r, ph2, blocks))
                    back_ref[...] -= 2.0 * there * term


def column(mask_ref, r, block, j, first, rest):
    bands = []
    for m in range(4):
        part = first[4 + j] if m == 0 else rest[j % 2, (m - 1) * BAND : m * BAND]
        bands.append(part * pattern_of(mask_ref, band_blocks(r, m), [block]))
    return beside(jnp.concatenate(bands, axis=0))


def last_kernel(
    mask_ref, prow, hrow, pcol, ss, so, s_lo, s_hi, o_lo, o_hi, ph2, send_ref, q1, q23,
    ph_ref, part_ref, php_ref, grad_ref, qcol, acc,
):
    r, c = lax.axis_index("row"), lax.axis_index("col")
    own = pattern_of(mask_ref, band_blocks(r, 0), [c])
    hp = send_ref[0:BAND]

    @pl.when(is_middle(r))
    def _():
        php_ref[...] = part_ref[...]
        acc[...] = dot_parts(prow[...], ph2[...])

    @pl.when(jnp.logical_not(is_middle(r)))
    def _():
        parts = (hp, q1[0:BAND], q23[0:BAND], q23[BAND:])
        php_ref[...] = php_of(mask_ref, r, c, parts, prow, qcol)
        acc[...] = jnp.zeros_like(acc)

    acc[...] += dot_parts(stacked(hp), rows_at(r, pcol, [c]))
    for flip, first, rests in ((0, ss, (s_lo, s_hi)), (1, so, (o_lo, o_hi))):
        for j in range(1 - flip, 4):
            block = jnp.bitwise_xor(c, 2 * j + flip)

            @pl.when(mask_ref[block, c] != 0)
            def _(first=first, rest=rests[j // 2], j=j, block=block):
                cols = column(mask_ref, r, block, j, first, rest)
                rows = dot_parts(hrow[...], cols)
                rows = rows * pattern_of(mask_ref, band_blocks(r, 0), [block])
                acc[...] += dot_parts(stacked(rows), rows_at(r, pcol, [block]))

    grad_ref[...] = 3.0 * (hp + ph_ref[...]) - 2.0 * (php_ref[...] + own * acc[...])


def call(kernel, outs, scratch, flops, *args):
    smem, vmem = pl.BlockSpec(memory_space=pltpu.SMEM), pl.BlockSpec(memory_space=pltpu.VMEM)
    moved = sum(a.size * a.dtype.itemsize for a in (*args, *outs))
    return pl.pallas_call(
        kernel,
        out_shape=outs,
        in_specs=[smem] + [vmem] * (len(args) - 1),
        out_specs=tuple(vmem for _ in outs),
        scratch_shapes=scratch,
        cost_estimate=pl.CostEstimate(flops=flops, bytes_accessed=moved, transcendentals=0),
        compiler_params=pltpu.CompilerParams(vmem_limit_bytes=VMEM_LIMIT),
    )(*args)


def to_middle(x):
    routes = [
        [(0, 1), (3, 2), (1, 0), (2, 3)],
        [(0, 2), (3, 1), (1, 0), (2, 3)],
        [(1, 2), (2, 1), (0, 0), (3, 3)],
    ]
    return [lax.ppermute(x, "row", pairs) for pairs in routes]


def whole_body(density, hamiltonian, block_mask):
    f32, bf16 = jnp.float32, jnp.bfloat16
    rows, cols = density.shape
    order = rows * ROWS

    def shape(a, b, dtype=bf16):
        return jax.ShapeDtypeStruct((a, b), dtype)

    tile, strip = shape(rows, cols, f32), shape(order, cols, f32)
    rows2, cols2 = shape(2 * rows, order), shape(order, 2 * cols)
    weight = 6 * rows * order * order
    p0, h0 = density, hamiltonian
    hx, py = swap(h0, "col", 2), swap(p0, "col", 4)
    p3 = swap(p0, "row", 3)
    both = lax.optimization_barrier(jnp.concatenate([p0, h0], axis=0))
    p0, h0 = both[:rows], both[rows:]
    p1, p2 = swap(p0, "row", 1), swap(p0, "row", 2)
    hy = swap(jnp.concatenate([h0, hx], axis=0), "col", 4)
    px = swap(jnp.concatenate([p0, py], axis=0), "col", 2)
    p1, p2, p3, hy, px = lax.optimization_barrier((p1, p2, p3, hy, px))
    ss = jnp.stack([h0, hx, hy[:rows], hy[rows:], p0, px[:rows], py, px[rows:]])
    so = swap(ss, "col", 1)

    b = jnp.concatenate([p1, p2, p3], axis=0)
    half = b.shape[0] // 2
    upper, lower = b[:half], b[half:]
    ux, ly = swap(upper, "col", 2), swap(lower, "col", 4)

    part, pcol = call(start_kernel, (tile, cols2), [], weight, block_mask, p0, p1, p2, p3, ss)
    send, mark = call(
        hp_kernel, (shape(2 * rows, cols, f32), shape(8, cols, f32)), [], weight,
        block_mask, part, pcol, ss, so,
    )
    ux, ly, mark = lax.optimization_barrier((ux, ly, mark))
    q1, q2, q3 = to_middle(send)
    uy = swap(jnp.concatenate([upper, ux], axis=0), "col", 4)
    lx = swap(jnp.concatenate([lower, ly], axis=0), "col", 2)
    hrow, prow, hp = call(
        rows_kernel, (rows2, rows2, tile), [], weight, block_mask, ss, so, send, mark
    )
    hcol, across = call(
        h_kernel, (cols2, shape(2 * rows, cols, f32)), [], AHEAD * weight,
        block_mask, q3, q1, q2, send,
    )
    q23 = swap(across, "row", 1)
    uy, lx, hcol = lax.optimization_barrier((uy, lx, hcol))
    s_lo = jnp.stack([b, jnp.concatenate([ux, lx[:half]], axis=0)])
    s_hi = jnp.stack([jnp.concatenate(pair, axis=0) for pair in ((uy[:half], ly), (uy[half:], lx[half:]))])
    o_lo, o_hi = swap(s_lo, "col", 1), swap(s_hi, "col", 1)

    far = shape(2 * rows, order // 4)
    part, own_lo, own_hi, php = call(
        own_kernel, (strip, far, far, tile), [pltpu.VMEM((order, 2 * cols), bf16)],
        AHEAD * weight, block_mask, hcol, ss, s_lo, s_hi, prow, send, q1, q2, q3,
    )
    part, other_hi = call(
        other_kernel, (strip, far), [], weight, block_mask, hcol, so, o_hi, part
    )
    back, ph, ph2 = call(
        ph_kernel, (tile, tile, cols2),
        [pltpu.VMEM((order, cols), f32), pltpu.VMEM((2 * rows, order // 4), bf16)], weight,
        block_mask, hcol, so, o_lo, part, own_lo, own_hi, other_hi,
    )
    got = swap(back, "row", 1)
    php, grad = call(
        last_kernel, (tile, tile),
        [pltpu.VMEM((order, 2 * cols), bf16), pltpu.VMEM((rows, cols), f32)], weight,
        block_mask, prow, hrow, pcol, ss, so, s_lo, s_hi, o_lo, o_hi, ph2, send, q1, q23, ph, php,
    )
    return hp, php, grad + got


def body(density, hamiltonian, block_mask, shape):
    tile_rows, tile_cols = density.shape
    if shape == (ROWS, COLS) and tile_rows == 2 * BLK and tile_cols == BLK:
        return whole_body(density, hamiltonian, block_mask)
    return strips_body(density, hamiltonian, block_mask)


def solution(mesh):
    placed = (P("row", "col"), P("row", "col"), P())
    return jax.shard_map(
        functools.partial(body, shape=(mesh.shape["row"], mesh.shape["col"])),
        mesh=mesh,
        in_specs=placed,
        out_specs=(P("row", "col"), P("row", "col"), P("row", "col")),
        check_vma=False,
    )
```

```python
import functools

import jax
import jax.numpy as jnp
from jax import lax
from jax.experimental import pallas as pl
from jax.experimental.pallas import tpu as pltpu
from jax.sharding import PartitionSpec as P

BLK = 128
VMEM_LIMIT = 40 * 1024 * 1024
AHEAD = 8

highest = lax.Precision.HIGHEST


def product(leading, second):
    return jnp.dot(leading, second, precision=highest, preferred_element_type=jnp.float32)


def tile_pattern(block_mask, row_index, col_index, tile_rows, tile_cols):
    row_blocks = (row_index * tile_rows + jnp.arange(tile_rows, dtype=jnp.int32)) // BLK
    col_blocks = (col_index * tile_cols + jnp.arange(tile_cols, dtype=jnp.int32)) // BLK
    block_ids = jnp.arange(block_mask.shape[0], dtype=jnp.int32)
    row_hot = (row_blocks[:, None] == block_ids[None, :]).astype(jnp.float32)
    col_hot = (col_blocks[:, None] == block_ids[None, :]).astype(jnp.float32)
    return product(product(row_hot, block_mask.astype(jnp.float32)), col_hot.T)


def strips_body(density, hamiltonian, block_mask):
    row_index = lax.axis_index("row")
    col_index = lax.axis_index("col")
    pattern = tile_pattern(block_mask, row_index, col_index, *density.shape)
    kept_density = density * pattern
    kept_hamiltonian = hamiltonian * pattern
    density_rows = lax.all_gather(kept_density, "col", axis=1, tiled=True)
    hamiltonian_rows = lax.all_gather(kept_hamiltonian, "col", axis=1, tiled=True)
    density_strip = lax.all_gather(kept_density, "row", axis=0, tiled=True)
    hamiltonian_strip = lax.all_gather(kept_hamiltonian, "row", axis=0, tiled=True)
    hp_product = product(hamiltonian_rows, density_strip) * pattern
    ph_product = product(density_rows, hamiltonian_strip) * pattern
    hp_strip = lax.all_gather(hp_product, "row", axis=0, tiled=True)
    ph_strip = lax.all_gather(ph_product, "row", axis=0, tiled=True)
    hp_rows = lax.all_gather(hp_product, "col", axis=1, tiled=True)
    php_product = product(density_rows, hp_strip) * pattern
    pph_product = product(density_rows, ph_strip) * pattern
    hpp_product = product(hp_rows, density_strip) * pattern
    gradient = pattern * (
        3.0 * (hp_product + ph_product) - 2.0 * (php_product + pph_product + hpp_product)
    )
    return (hp_product, php_product, gradient)


ROWS, COLS = 4, 8


def swap(x, axis, mask):
    size = ROWS if axis == "row" else COLS
    return lax.ppermute(x, axis, [(i, i ^ mask) for i in range(size)])


def after(value, *others):
    return lax.optimization_barrier((value, *others))[0]


def split(x):
    high = x.astype(jnp.bfloat16)
    return high, (x - high.astype(jnp.float32)).astype(jnp.bfloat16)


def stacked(x):
    return jnp.concatenate(split(x), axis=0)


def beside(x):
    return jnp.concatenate(split(x), axis=1)


def mul(a, b):
    return jnp.dot(a, b, preferred_element_type=jnp.float32)


def dot_parts(a, b):
    t = mul(a, b)
    m, n = t.shape[0] // 2, t.shape[1] // 2
    return (t[:m, :n] + (t[:m, n:] + t[m:, :n])) + t[m:, n:]


def dot_wide(a, b):
    t = mul(a, b[0])
    m = t.shape[0] // 2
    return t[:m] + (t[m:] + mul(a[:m], b[1]))


def dot_tall(a, b):
    t = mul(a[0], b)
    n = t.shape[1] // 2
    return t[:, :n] + (t[:, n:] + mul(a[1], b[:, :n]))


def place(r, col_block):
    band = jnp.bitwise_xor(lax.shift_right_logical(col_block, 1), r)
    start = band * (2 * BLK) + jnp.bitwise_and(col_block, 1) * BLK
    return pl.multiple_of(start, BLK)


def block_at(r, position):
    return 2 * jnp.bitwise_xor(position // 2, r) + position % 2


def pattern_of(mask_ref, row_blocks, col_blocks):
    rows = []
    for i in row_blocks:
        rows.append(
            jnp.concatenate(
                [jnp.full((BLK, BLK), mask_ref[i, j].astype(jnp.float32)) for j in col_blocks],
                axis=1,
            )
        )
    return jnp.concatenate(rows, axis=0)


def band_blocks(r, m):
    return [block_at(r, 2 * m), block_at(r, 2 * m + 1)]


BAND = 2 * BLK


def fill_rows(mask_ref, r, c, ss, so, first, out):
    for j in range(4):
        for flip, ref in ((0, ss), (1, so)):
            block = jnp.bitwise_xor(c, 2 * j + flip)
            part = ref[first + j] * pattern_of(mask_ref, band_blocks(r, 0), [block])
            out[:, pl.ds(place(r, block), BLK)] = stacked(part)


def fill_cols(mask_ref, r, c, parts, out):
    for m, part in enumerate(parts):
        kept = part * pattern_of(mask_ref, band_blocks(r, m), [c])
        out[m * BAND : (m + 1) * BAND, :] = beside(kept)


def left_pair(mask_ref, r, blocks, first, at):
    parts = [
        first[at + i] * pattern_of(mask_ref, band_blocks(r, 0), [blocks[i]]) for i in (0, 1)
    ]
    return stacked(jnp.concatenate(parts, axis=1))


def pairs(c, flip):
    for j in (0, 2):
        yield j, [jnp.bitwise_xor(c, 2 * (j + i) + flip) for i in (0, 1)]


def start_kernel(mask_ref, p0, p1, p3, p2, ss, part_ref, pcol):
    r, c = lax.axis_index("row"), lax.axis_index("col")
    fill_cols(mask_ref, r, c, (p0[...], p1[...], p2[...], p3[...]), pcol)
    total = jnp.zeros(part_ref.shape, jnp.float32)
    for j, blocks in pairs(c, 0):
        total += dot_parts(left_pair(mask_ref, r, blocks, ss, j), rows_at(r, pcol, blocks))
    part_ref[...] = total


def hp_kernel(mask_ref, part_ref, pcol, ss, so, send_ref, mark_ref):
    r, c = lax.axis_index("row"), lax.axis_index("col")
    total = part_ref[...]
    for j, blocks in pairs(c, 1):
        total += dot_parts(left_pair(mask_ref, r, blocks, so, j), rows_at(r, pcol, blocks))
    own = pattern_of(mask_ref, band_blocks(r, 0), [c])
    send_ref[0:BAND] = total * own
    send_ref[BAND:] = ss[0] * own
    mark_ref[...] = jnp.zeros_like(mark_ref)


def rows_kernel(mask_ref, ss, so, send_ref, mark_ref, hrow, prow, hp_ref):
    r, c = lax.axis_index("row"), lax.axis_index("col")
    hp_ref[...] = send_ref[0:BAND]
    fill_rows(mask_ref, r, c, ss, so, 0, hrow)
    fill_rows(mask_ref, r, c, ss, so, 4, prow)


def is_middle(r):
    return jnp.logical_or(r == 1, r == 2)


def column_pair(mask_ref, r, blocks, j, first, rest):
    bands = []
    for m in range(4):
        parts = []
        for i in (0, 1):
            part = first[4 + j + i] if m == 0 else rest[i, (m - 1) * BAND : m * BAND]
            parts.append(part * pattern_of(mask_ref, band_blocks(r, m), [blocks[i]]))
        bands.append(jnp.concatenate(parts, axis=1))
    return split(jnp.concatenate(bands, axis=0))


def rows_at(r, ref, blocks):
    return jnp.concatenate([ref[pl.ds(place(r, b), BLK), :] for b in blocks], axis=0)


def far_rows(cols):
    return jnp.concatenate([part[BAND : 2 * BAND] for part in cols], axis=0)


def h_kernel(mask_ref, q0, q1, q3, q2, hcol, across_ref):
    r, c = lax.axis_index("row"), lax.axis_index("col")
    fill_cols(mask_ref, r, c, [ref[BAND:] for ref in (q0, q1, q2, q3)], hcol)
    across_ref[0:BAND] = q3[0:BAND]
    across_ref[BAND:] = q2[0:BAND]


def any_live(mask_ref, blocks, c):
    return sum(mask_ref[b, c] for b in blocks) != 0


def add_ph(mask_ref, r, c, pair, first, rest, hcol, ph_ref, far):
    j, blocks = pair

    @pl.when(any_live(mask_ref, blocks, c))
    def _():
        cols = column_pair(mask_ref, r, blocks, j, first, rest)
        ph_ref[...] += dot_tall(cols, rows_at(r, hcol, blocks))
        far[...] = far_rows(cols)


def own_kernel(mask_ref, hcol, ss, lo, hi, ph_ref, far_lo, far_hi):
    r, c = lax.axis_index("row"), lax.axis_index("col")

    @pl.when(is_middle(r))
    def _():
        ph_ref[...] = jnp.zeros_like(ph_ref)
        for pair, rest, far in zip(pairs(c, 0), (lo, hi), (far_lo, far_hi)):
            add_ph(mask_ref, r, c, pair, ss, rest, hcol, ph_ref, far)


def other_kernel(mask_ref, hcol, so, hi, part_ref, ph_ref, far):
    r, c = lax.axis_index("row"), lax.axis_index("col")

    @pl.when(is_middle(r))
    def _():
        ph_ref[...] = part_ref[...]
        _, pair = pairs(c, 1)
        add_ph(mask_ref, r, c, pair, so, hi, hcol, ph_ref, far)


def ph_kernel(
    mask_ref, hcol, so, lo, part_ref, own_lo, own_hi, other_hi, back_ref, tile_ref, ph2,
    ph_ref, other_lo,
):
    r, c = lax.axis_index("row"), lax.axis_index("col")
    back_ref[...] = jnp.zeros_like(back_ref)
    tile_ref[...] = jnp.zeros_like(tile_ref)
    ph2[...] = jnp.zeros_like(ph2)

    @pl.when(is_middle(r))
    def _():
        ph_ref[...] = part_ref[...]
        add_ph(mask_ref, r, c, next(pairs(c, 1)), so, lo, hcol, ph_ref, other_lo)
        for m in range(4):
            at = pl.ds(m * BAND, BAND)
            rows = ph_ref[at, :] * pattern_of(mask_ref, band_blocks(r, m), [c])
            ph2[at, :] = beside(rows)
            if m == 0:
                tile_ref[...] = rows
            if m == 1:
                back_ref[...] = 3.0 * rows
        there = pattern_of(mask_ref, band_blocks(r, 1), [c])
        fars = ((0, (own_lo, own_hi)), (1, (other_lo, other_hi)))
        for flip, parts in fars:
            for (_, blocks), far in zip(pairs(c, flip), parts):

                @pl.when(any_live(mask_ref, blocks, c))
                def _(blocks=blocks, far=far):
                    term = dot_parts(far[...], rows_at(r, ph2, blocks))
                    back_ref[...] -= 2.0 * there * term


def column(mask_ref, r, block, j, first, rest):
    bands = []
    for m in range(4):
        part = first[4 + j] if m == 0 else rest[j % 2, (m - 1) * BAND : m * BAND]
        bands.append(part * pattern_of(mask_ref, band_blocks(r, m), [block]))
    return beside(jnp.concatenate(bands, axis=0))


def last_kernel(
    mask_ref, prow, hrow, pcol, ss, so, s_lo, s_hi, o_lo, o_hi, ph2, send_ref, q1, q2, q3, q23,
    ph_ref, php_ref, grad_ref, qcol, acc,
):
    r, c = lax.axis_index("row"), lax.axis_index("col")
    own = pattern_of(mask_ref, band_blocks(r, 0), [c])
    hp = send_ref[0:BAND]

    for m, part in enumerate((hp, q1[0:BAND])):
        qcol[m * BAND : (m + 1) * BAND, :] = beside(part)

    @pl.when(is_middle(r))
    def _():
        for m, part in ((2, q2[0:BAND]), (3, q3[0:BAND])):
            qcol[m * BAND : (m + 1) * BAND, :] = beside(part)
        acc[...] = dot_parts(prow[...], ph2[...])

    @pl.when(jnp.logical_not(is_middle(r)))
    def _():
        for m, part in ((2, q23[0:BAND]), (3, q23[BAND:])):
            qcol[m * BAND : (m + 1) * BAND, :] = beside(part)
        acc[...] = jnp.zeros_like(acc)

    php = dot_parts(prow[...], qcol[...]) * own
    php_ref[...] = php
    acc[...] += dot_parts(stacked(hp), rows_at(r, pcol, [c]))
    for flip, first, rests in ((0, ss, (s_lo, s_hi)), (1, so, (o_lo, o_hi))):
        for j in range(1 - flip, 4):
            block = jnp.bitwise_xor(c, 2 * j + flip)

            @pl.when(mask_ref[block, c] != 0)
            def _(first=first, rest=rests[j // 2], j=j, block=block):
                cols = column(mask_ref, r, block, j, first, rest)
                rows = dot_parts(hrow[...], cols)
                rows = rows * pattern_of(mask_ref, band_blocks(r, 0), [block])
                acc[...] += dot_parts(stacked(rows), rows_at(r, pcol, [block]))

    grad_ref[...] = 3.0 * (hp + ph_ref[...]) - 2.0 * (php + own * acc[...])


def call(kernel, outs, scratch, flops, *args):
    smem, vmem = pl.BlockSpec(memory_space=pltpu.SMEM), pl.BlockSpec(memory_space=pltpu.VMEM)
    moved = sum(a.size * a.dtype.itemsize for a in (*args, *outs))
    return pl.pallas_call(
        kernel,
        out_shape=outs,
        in_specs=[smem] + [vmem] * (len(args) - 1),
        out_specs=tuple(vmem for _ in outs),
        scratch_shapes=scratch,
        cost_estimate=pl.CostEstimate(flops=flops, bytes_accessed=moved, transcendentals=0),
        compiler_params=pltpu.CompilerParams(vmem_limit_bytes=VMEM_LIMIT),
    )(*args)


def to_middle(x):
    routes = [
        [(0, 1), (3, 2), (1, 0), (2, 3)],
        [(0, 2), (3, 1), (1, 0), (2, 3)],
        [(1, 2), (2, 1), (0, 0), (3, 3)],
    ]
    return [lax.ppermute(x, "row", pairs) for pairs in routes]


def whole_body(density, hamiltonian, block_mask):
    f32, bf16 = jnp.float32, jnp.bfloat16
    rows, cols = density.shape
    order = rows * ROWS

    def shape(a, b, dtype=bf16):
        return jax.ShapeDtypeStruct((a, b), dtype)

    tile, strip = shape(rows, cols, f32), shape(order, cols, f32)
    rows2, cols2 = shape(2 * rows, order), shape(order, 2 * cols)
    weight = 6 * rows * order * order
    p0, h0 = density, hamiltonian
    hx, py = swap(h0, "col", 2), swap(p0, "col", 4)
    p3 = swap(p0, "row", 3)
    both = lax.optimization_barrier(jnp.concatenate([p0, h0], axis=0))
    p0, h0 = both[:rows], both[rows:]
    p1 = swap(p0, "row", 1)
    p2 = swap(p0, "row", 2)
    hy = swap(jnp.concatenate([h0, hx], axis=0), "col", 4)
    px = swap(jnp.concatenate([p0, py], axis=0), "col", 2)
    px, p1, hy, p2, p3 = lax.optimization_barrier((px, p1, hy, p2, p3))
    ss = jnp.stack([h0, hx, hy[:rows], hy[rows:], p0, px[:rows], py, px[rows:]])
    so = swap(ss, "col", 1)

    b = jnp.concatenate([p1, p2, p3], axis=0)
    half = b.shape[0] // 2
    upper, lower = b[:half], b[half:]
    ux, ly = swap(upper, "col", 2), swap(lower, "col", 4)

    part, pcol = call(start_kernel, (tile, cols2), [], weight, block_mask, p0, p1, p3, p2, ss)
    send, mark = call(
        hp_kernel, (shape(2 * rows, cols, f32), shape(8, cols, f32)), [], weight,
        block_mask, part, pcol, ss, so,
    )
    ly, ux, mark = lax.optimization_barrier((ly, ux, mark))
    q1, q2, q3 = to_middle(send)
    uy = swap(jnp.concatenate([upper, ux], axis=0), "col", 4)
    lx = swap(jnp.concatenate([lower, ly], axis=0), "col", 2)
    hrow, prow, hp = call(
        rows_kernel, (rows2, rows2, tile), [], weight, block_mask, ss, so, send, mark
    )
    hcol, across = call(
        h_kernel, (cols2, shape(2 * rows, cols, f32)), [], AHEAD * weight,
        block_mask, send, q1, q3, q2,
    )
    q23 = swap(across, "row", 1)
    lx, uy, hcol = lax.optimization_barrier((lx, uy, hcol))
    s_lo = jnp.stack([b, jnp.concatenate([ux, lx[:half]], axis=0)])
    s_hi = jnp.stack([jnp.concatenate(pair, axis=0) for pair in ((uy[:half], ly), (uy[half:], lx[half:]))])
    o_lo, o_hi = swap(s_lo, "col", 1), swap(s_hi, "col", 1)

    far = shape(2 * rows, order // 4)
    part, own_lo, own_hi = call(
        own_kernel, (strip, far, far), [], AHEAD * weight, block_mask, hcol, ss, s_lo, s_hi
    )
    part, other_hi = call(
        other_kernel, (strip, far), [], weight, block_mask, hcol, so, o_hi, part
    )
    back, ph, ph2 = call(
        ph_kernel, (tile, tile, cols2),
        [pltpu.VMEM((order, cols), f32), pltpu.VMEM((2 * rows, order // 4), bf16)], weight,
        block_mask, hcol, so, o_lo, part, own_lo, own_hi, other_hi,
    )
    got = swap(back, "row", 1)
    php, grad = call(
        last_kernel, (tile, tile),
        [pltpu.VMEM((order, 2 * cols), bf16), pltpu.VMEM((rows, cols), f32)], weight,
        block_mask, prow, hrow, pcol, ss, so, s_lo, s_hi, o_lo, o_hi, ph2, send, q1, q2, q3, q23,
        ph,
    )
    return hp, php, grad + got


def body(density, hamiltonian, block_mask, shape):
    tile_rows, tile_cols = density.shape
    if shape == (ROWS, COLS) and tile_rows == 2 * BLK and tile_cols == BLK:
        return whole_body(density, hamiltonian, block_mask)
    return strips_body(density, hamiltonian, block_mask)


def solution(mesh):
    placed = (P("row", "col"), P("row", "col"), P())
    return jax.shard_map(
        functools.partial(body, shape=(mesh.shape["row"], mesh.shape["col"])),
        mesh=mesh,
        in_specs=placed,
        out_specs=(P("row", "col"), P("row", "col"), P("row", "col")),
        check_vma=False,
    )
```

```python
import functools

import jax
import jax.numpy as jnp
from jax import lax
from jax.experimental import pallas as pl
from jax.experimental.pallas import tpu as pltpu
from jax.sharding import PartitionSpec as P

BLK = 128
VMEM_LIMIT = 40 * 1024 * 1024
AHEAD = 8

highest = lax.Precision.HIGHEST


def product(leading, second):
    return jnp.dot(leading, second, precision=highest, preferred_element_type=jnp.float32)


def tile_pattern(block_mask, row_index, col_index, tile_rows, tile_cols):
    row_blocks = (row_index * tile_rows + jnp.arange(tile_rows, dtype=jnp.int32)) // BLK
    col_blocks = (col_index * tile_cols + jnp.arange(tile_cols, dtype=jnp.int32)) // BLK
    block_ids = jnp.arange(block_mask.shape[0], dtype=jnp.int32)
    row_hot = (row_blocks[:, None] == block_ids[None, :]).astype(jnp.float32)
    col_hot = (col_blocks[:, None] == block_ids[None, :]).astype(jnp.float32)
    return product(product(row_hot, block_mask.astype(jnp.float32)), col_hot.T)


def strips_body(density, hamiltonian, block_mask):
    row_index = lax.axis_index("row")
    col_index = lax.axis_index("col")
    pattern = tile_pattern(block_mask, row_index, col_index, *density.shape)
    kept_density = density * pattern
    kept_hamiltonian = hamiltonian * pattern
    density_rows = lax.all_gather(kept_density, "col", axis=1, tiled=True)
    hamiltonian_rows = lax.all_gather(kept_hamiltonian, "col", axis=1, tiled=True)
    density_strip = lax.all_gather(kept_density, "row", axis=0, tiled=True)
    hamiltonian_strip = lax.all_gather(kept_hamiltonian, "row", axis=0, tiled=True)
    hp_product = product(hamiltonian_rows, density_strip) * pattern
    ph_product = product(density_rows, hamiltonian_strip) * pattern
    hp_strip = lax.all_gather(hp_product, "row", axis=0, tiled=True)
    ph_strip = lax.all_gather(ph_product, "row", axis=0, tiled=True)
    hp_rows = lax.all_gather(hp_product, "col", axis=1, tiled=True)
    php_product = product(density_rows, hp_strip) * pattern
    pph_product = product(density_rows, ph_strip) * pattern
    hpp_product = product(hp_rows, density_strip) * pattern
    gradient = pattern * (
        3.0 * (hp_product + ph_product) - 2.0 * (php_product + pph_product + hpp_product)
    )
    return (hp_product, php_product, gradient)


ROWS, COLS = 4, 8


def swap(x, axis, mask):
    size = ROWS if axis == "row" else COLS
    return lax.ppermute(x, axis, [(i, i ^ mask) for i in range(size)])


def after(value, *others):
    return lax.optimization_barrier((value, *others))[0]


def split(x):
    high = x.astype(jnp.bfloat16)
    return high, (x - high.astype(jnp.float32)).astype(jnp.bfloat16)


def stacked(x):
    return jnp.concatenate(split(x), axis=0)


def beside(x):
    return jnp.concatenate(split(x), axis=1)


def mul(a, b):
    return jnp.dot(a, b, preferred_element_type=jnp.float32)


def dot_parts(a, b):
    t = mul(a, b)
    m, n = t.shape[0] // 2, t.shape[1] // 2
    return (t[:m, :n] + (t[:m, n:] + t[m:, :n])) + t[m:, n:]


def dot_wide(a, b):
    t = mul(a, b[0])
    m = t.shape[0] // 2
    return t[:m] + (t[m:] + mul(a[:m], b[1]))


def dot_tall(a, b):
    t = mul(a[0], b)
    n = t.shape[1] // 2
    return t[:, :n] + (t[:, n:] + mul(a[1], b[:, :n]))


def place(r, col_block):
    band = jnp.bitwise_xor(lax.shift_right_logical(col_block, 1), r)
    start = band * (2 * BLK) + jnp.bitwise_and(col_block, 1) * BLK
    return pl.multiple_of(start, BLK)


def block_at(r, position):
    return 2 * jnp.bitwise_xor(position // 2, r) + position % 2


def pattern_of(mask_ref, row_blocks, col_blocks):
    rows = []
    for i in row_blocks:
        rows.append(
            jnp.concatenate(
                [jnp.full((BLK, BLK), mask_ref[i, j].astype(jnp.float32)) for j in col_blocks],
                axis=1,
            )
        )
    return jnp.concatenate(rows, axis=0)


def band_blocks(r, m):
    return [block_at(r, 2 * m), block_at(r, 2 * m + 1)]


BAND = 2 * BLK


def fill_rows(mask_ref, r, c, ss, so, first, out):
    for j in range(4):
        for flip, ref in ((0, ss), (1, so)):
            block = jnp.bitwise_xor(c, 2 * j + flip)
            part = ref[first + j] * pattern_of(mask_ref, band_blocks(r, 0), [block])
            out[:, pl.ds(place(r, block), BLK)] = stacked(part)


def fill_cols(mask_ref, r, c, parts, out):
    for m, part in enumerate(parts):
        kept = part * pattern_of(mask_ref, band_blocks(r, m), [c])
        out[m * BAND : (m + 1) * BAND, :] = beside(kept)


def left_pair(mask_ref, r, blocks, first, at):
    parts = [
        first[at + i] * pattern_of(mask_ref, band_blocks(r, 0), [blocks[i]]) for i in (0, 1)
    ]
    return stacked(jnp.concatenate(parts, axis=1))


def pairs(c, flip):
    for j in (0, 2):
        yield j, [jnp.bitwise_xor(c, 2 * (j + i) + flip) for i in (0, 1)]


def start_kernel(mask_ref, p0, p1, p3, p2, ss, part_ref, pcol):
    r, c = lax.axis_index("row"), lax.axis_index("col")
    fill_cols(mask_ref, r, c, (p0[...], p1[...], p2[...], p3[...]), pcol)
    total = jnp.zeros(part_ref.shape, jnp.float32)
    for j, blocks in pairs(c, 0):
        total += dot_parts(left_pair(mask_ref, r, blocks, ss, j), rows_at(r, pcol, blocks))
    part_ref[...] = total


def hp_kernel(mask_ref, part_ref, pcol, ss, so, send_ref, mark_ref):
    r, c = lax.axis_index("row"), lax.axis_index("col")
    total = part_ref[...]
    for j, blocks in pairs(c, 1):
        total += dot_parts(left_pair(mask_ref, r, blocks, so, j), rows_at(r, pcol, blocks))
    own = pattern_of(mask_ref, band_blocks(r, 0), [c])
    send_ref[0:BAND] = total * own
    send_ref[BAND:] = ss[0] * own
    mark_ref[...] = jnp.zeros_like(mark_ref)


def rows_kernel(mask_ref, ss, so, send_ref, mark_ref, hrow, prow, hp_ref):
    r, c = lax.axis_index("row"), lax.axis_index("col")
    hp_ref[...] = send_ref[0:BAND]
    fill_rows(mask_ref, r, c, ss, so, 0, hrow)
    fill_rows(mask_ref, r, c, ss, so, 4, prow)


def is_middle(r):
    return jnp.logical_or(r == 1, r == 2)


def column_pair(mask_ref, r, blocks, j, first, rest):
    bands = []
    for m in range(4):
        parts = []
        for i in (0, 1):
            part = first[4 + j + i] if m == 0 else rest[i, (m - 1) * BAND : m * BAND]
            parts.append(part * pattern_of(mask_ref, band_blocks(r, m), [blocks[i]]))
        bands.append(jnp.concatenate(parts, axis=1))
    return split(jnp.concatenate(bands, axis=0))


def rows_at(r, ref, blocks):
    return jnp.concatenate([ref[pl.ds(place(r, b), BLK), :] for b in blocks], axis=0)


def far_rows(cols):
    return jnp.concatenate([part[BAND : 2 * BAND] for part in cols], axis=0)


def h_kernel(mask_ref, q0, q1, q3, q2, hcol, across_ref):
    r, c = lax.axis_index("row"), lax.axis_index("col")
    fill_cols(mask_ref, r, c, [ref[BAND:] for ref in (q0, q1, q2, q3)], hcol)
    across_ref[0:BAND] = q3[0:BAND]
    across_ref[BAND:] = q2[0:BAND]


def any_live(mask_ref, blocks, c):
    return sum(mask_ref[b, c] for b in blocks) != 0


def add_ph(mask_ref, r, c, pair, first, rest, hcol, ph_ref, far):
    j, blocks = pair

    @pl.when(any_live(mask_ref, blocks, c))
    def _():
        cols = column_pair(mask_ref, r, blocks, j, first, rest)
        ph_ref[...] += dot_tall(cols, rows_at(r, hcol, blocks))
        far[...] = far_rows(cols)


def own_kernel(mask_ref, hcol, ss, lo, hi, ph_ref, far_lo, far_hi):
    r, c = lax.axis_index("row"), lax.axis_index("col")

    @pl.when(is_middle(r))
    def _():
        ph_ref[...] = jnp.zeros_like(ph_ref)
        for pair, rest, far in zip(pairs(c, 0), (lo, hi), (far_lo, far_hi)):
            add_ph(mask_ref, r, c, pair, ss, rest, hcol, ph_ref, far)


def other_kernel(mask_ref, hcol, so, hi, part_ref, ph_ref, far):
    r, c = lax.axis_index("row"), lax.axis_index("col")

    @pl.when(is_middle(r))
    def _():
        ph_ref[...] = part_ref[...]
        _, pair = pairs(c, 1)
        add_ph(mask_ref, r, c, pair, so, hi, hcol, ph_ref, far)


def ph_kernel(
    mask_ref, hcol, so, lo, part_ref, own_lo, own_hi, other_hi, back_ref, tile_ref, ph2,
    ph_ref, other_lo,
):
    r, c = lax.axis_index("row"), lax.axis_index("col")
    back_ref[...] = jnp.zeros_like(back_ref)
    tile_ref[...] = jnp.zeros_like(tile_ref)
    ph2[...] = jnp.zeros_like(ph2)

    @pl.when(is_middle(r))
    def _():
        ph_ref[...] = part_ref[...]
        add_ph(mask_ref, r, c, next(pairs(c, 1)), so, lo, hcol, ph_ref, other_lo)
        for m in range(4):
            at = pl.ds(m * BAND, BAND)
            rows = ph_ref[at, :] * pattern_of(mask_ref, band_blocks(r, m), [c])
            ph2[at, :] = beside(rows)
            if m == 0:
                tile_ref[...] = rows
            if m == 1:
                back_ref[...] = 3.0 * rows
        there = pattern_of(mask_ref, band_blocks(r, 1), [c])
        fars = ((0, (own_lo, own_hi)), (1, (other_lo, other_hi)))
        for flip, parts in fars:
            for (_, blocks), far in zip(pairs(c, flip), parts):

                @pl.when(any_live(mask_ref, blocks, c))
                def _(blocks=blocks, far=far):
                    term = dot_parts(far[...], rows_at(r, ph2, blocks))
                    back_ref[...] -= 2.0 * there * term


def column(mask_ref, r, block, j, first, rest):
    bands = []
    for m in range(4):
        part = first[4 + j] if m == 0 else rest[j % 2, (m - 1) * BAND : m * BAND]
        bands.append(part * pattern_of(mask_ref, band_blocks(r, m), [block]))
    return beside(jnp.concatenate(bands, axis=0))


def last_kernel(
    mask_ref, prow, hrow, pcol, ss, so, s_lo, s_hi, o_lo, o_hi, ph2, send_ref, q1, q2, q3, q23,
    ph_ref, php_ref, grad_ref, qcol, acc,
):
    r, c = lax.axis_index("row"), lax.axis_index("col")
    own = pattern_of(mask_ref, band_blocks(r, 0), [c])
    hp = send_ref[0:BAND]

    for m, part in enumerate((hp, q1[0:BAND])):
        qcol[m * BAND : (m + 1) * BAND, :] = beside(part)

    @pl.when(is_middle(r))
    def _():
        for m, part in ((2, q2[0:BAND]), (3, q3[0:BAND])):
            qcol[m * BAND : (m + 1) * BAND, :] = beside(part)
        acc[...] = dot_parts(prow[...], ph2[...])

    @pl.when(jnp.logical_not(is_middle(r)))
    def _():
        for m, part in ((2, q23[0:BAND]), (3, q23[BAND:])):
            qcol[m * BAND : (m + 1) * BAND, :] = beside(part)
        acc[...] = jnp.zeros_like(acc)

    php = dot_parts(prow[...], qcol[...]) * own
    php_ref[...] = php
    acc[...] += dot_parts(stacked(hp), rows_at(r, pcol, [c]))
    for flip, first, rests in ((0, ss, (s_lo, s_hi)), (1, so, (o_lo, o_hi))):
        for j in range(1 - flip, 4):
            block = jnp.bitwise_xor(c, 2 * j + flip)

            met = any_live(mask_ref, band_blocks(r, 0), block)

            @pl.when(jnp.logical_and(mask_ref[block, c] != 0, met))
            def _(first=first, rest=rests[j // 2], j=j, block=block):
                cols = column(mask_ref, r, block, j, first, rest)
                rows = dot_parts(hrow[...], cols)
                rows = rows * pattern_of(mask_ref, band_blocks(r, 0), [block])
                acc[...] += dot_parts(stacked(rows), rows_at(r, pcol, [block]))

    grad_ref[...] = 3.0 * (hp + ph_ref[...]) - 2.0 * (php + own * acc[...])


def call(kernel, outs, scratch, flops, *args):
    smem, vmem = pl.BlockSpec(memory_space=pltpu.SMEM), pl.BlockSpec(memory_space=pltpu.VMEM)
    moved = sum(a.size * a.dtype.itemsize for a in (*args, *outs))
    return pl.pallas_call(
        kernel,
        out_shape=outs,
        in_specs=[smem] + [vmem] * (len(args) - 1),
        out_specs=tuple(vmem for _ in outs),
        scratch_shapes=scratch,
        cost_estimate=pl.CostEstimate(flops=flops, bytes_accessed=moved, transcendentals=0),
        compiler_params=pltpu.CompilerParams(vmem_limit_bytes=VMEM_LIMIT),
    )(*args)


def to_middle(x):
    routes = [
        [(0, 1), (3, 2), (1, 0), (2, 3)],
        [(0, 2), (3, 1), (1, 0), (2, 3)],
        [(1, 2), (2, 1), (0, 0), (3, 3)],
    ]
    return [lax.ppermute(x, "row", pairs) for pairs in routes]


def whole_body(density, hamiltonian, block_mask):
    f32, bf16 = jnp.float32, jnp.bfloat16
    rows, cols = density.shape
    order = rows * ROWS

    def shape(a, b, dtype=bf16):
        return jax.ShapeDtypeStruct((a, b), dtype)

    tile, strip = shape(rows, cols, f32), shape(order, cols, f32)
    rows2, cols2 = shape(2 * rows, order), shape(order, 2 * cols)
    weight = 6 * rows * order * order
    p0, h0 = density, hamiltonian
    hx, py = swap(h0, "col", 2), swap(p0, "col", 4)
    p3 = swap(p0, "row", 3)
    both = lax.optimization_barrier(jnp.concatenate([p0, h0], axis=0))
    p0, h0 = both[:rows], both[rows:]
    p1 = swap(p0, "row", 1)
    p2 = swap(p0, "row", 2)
    hy = swap(jnp.concatenate([h0, hx], axis=0), "col", 4)
    px = swap(jnp.concatenate([p0, py], axis=0), "col", 2)
    px, p1, hy, p2, p3 = lax.optimization_barrier((px, p1, hy, p2, p3))
    ss = jnp.stack([h0, hx, hy[:rows], hy[rows:], p0, px[:rows], py, px[rows:]])
    so = swap(ss, "col", 1)

    b = jnp.concatenate([p1, p2, p3], axis=0)
    half = b.shape[0] // 2
    upper, lower = b[:half], b[half:]
    ux, ly = swap(upper, "col", 2), swap(lower, "col", 4)

    part, pcol = call(start_kernel, (tile, cols2), [], weight, block_mask, p0, p1, p3, p2, ss)
    send, mark = call(
        hp_kernel, (shape(2 * rows, cols, f32), shape(8, cols, f32)), [], weight,
        block_mask, part, pcol, ss, so,
    )
    ly, ux, mark = lax.optimization_barrier((ly, ux, mark))
    q1, q2, q3 = to_middle(send)
    uy = swap(jnp.concatenate([upper, ux], axis=0), "col", 4)
    lx = swap(jnp.concatenate([lower, ly], axis=0), "col", 2)
    hrow, prow, hp = call(
        rows_kernel, (rows2, rows2, tile), [], weight, block_mask, ss, so, send, mark
    )
    hcol, across = call(
        h_kernel, (cols2, shape(2 * rows, cols, f32)), [], AHEAD * weight,
        block_mask, send, q1, q3, q2,
    )
    q23 = swap(across, "row", 1)
    lx, uy, hcol = lax.optimization_barrier((lx, uy, hcol))
    s_lo = jnp.stack([b, jnp.concatenate([ux, lx[:half]], axis=0)])
    s_hi = jnp.stack([jnp.concatenate(pair, axis=0) for pair in ((uy[:half], ly), (uy[half:], lx[half:]))])
    o_lo, o_hi = swap(s_lo, "col", 1), swap(s_hi, "col", 1)

    far = shape(2 * rows, order // 4)
    part, own_lo, own_hi = call(
        own_kernel, (strip, far, far), [], AHEAD * weight, block_mask, hcol, ss, s_lo, s_hi
    )
    part, other_hi = call(
        other_kernel, (strip, far), [], weight, block_mask, hcol, so, o_hi, part
    )
    back, ph, ph2 = call(
        ph_kernel, (tile, tile, cols2),
        [pltpu.VMEM((order, cols), f32), pltpu.VMEM((2 * rows, order // 4), bf16)], weight,
        block_mask, hcol, so, o_lo, part, own_lo, own_hi, other_hi,
    )
    got = swap(back, "row", 1)
    php, grad = call(
        last_kernel, (tile, tile),
        [pltpu.VMEM((order, 2 * cols), bf16), pltpu.VMEM((rows, cols), f32)], weight,
        block_mask, prow, hrow, pcol, ss, so, s_lo, s_hi, o_lo, o_hi, ph2, send, q1, q2, q3, q23,
        ph,
    )
    return hp, php, grad + got


def body(density, hamiltonian, block_mask, shape):
    tile_rows, tile_cols = density.shape
    if shape == (ROWS, COLS) and tile_rows == 2 * BLK and tile_cols == BLK:
        return whole_body(density, hamiltonian, block_mask)
    return strips_body(density, hamiltonian, block_mask)


def solution(mesh):
    placed = (P("row", "col"), P("row", "col"), P())
    return jax.shard_map(
        functools.partial(body, shape=(mesh.shape["row"], mesh.shape["col"])),
        mesh=mesh,
        in_specs=placed,
        out_specs=(P("row", "col"), P("row", "col"), P("row", "col")),
        check_vma=False,
    )
```

```python
import functools

import jax
import jax.numpy as jnp
from jax import lax
from jax.experimental import pallas as pl
from jax.experimental.pallas import tpu as pltpu
from jax.sharding import PartitionSpec as P

BLK = 128
VMEM_LIMIT = 40 * 1024 * 1024
AHEAD = 8

highest = lax.Precision.HIGHEST


def product(leading, second):
    return jnp.dot(leading, second, precision=highest, preferred_element_type=jnp.float32)


def tile_pattern(block_mask, row_index, col_index, tile_rows, tile_cols):
    row_blocks = (row_index * tile_rows + jnp.arange(tile_rows, dtype=jnp.int32)) // BLK
    col_blocks = (col_index * tile_cols + jnp.arange(tile_cols, dtype=jnp.int32)) // BLK
    block_ids = jnp.arange(block_mask.shape[0], dtype=jnp.int32)
    row_hot = (row_blocks[:, None] == block_ids[None, :]).astype(jnp.float32)
    col_hot = (col_blocks[:, None] == block_ids[None, :]).astype(jnp.float32)
    return product(product(row_hot, block_mask.astype(jnp.float32)), col_hot.T)


def strips_body(density, hamiltonian, block_mask):
    row_index = lax.axis_index("row")
    col_index = lax.axis_index("col")
    pattern = tile_pattern(block_mask, row_index, col_index, *density.shape)
    kept_density = density * pattern
    kept_hamiltonian = hamiltonian * pattern
    density_rows = lax.all_gather(kept_density, "col", axis=1, tiled=True)
    hamiltonian_rows = lax.all_gather(kept_hamiltonian, "col", axis=1, tiled=True)
    density_strip = lax.all_gather(kept_density, "row", axis=0, tiled=True)
    hamiltonian_strip = lax.all_gather(kept_hamiltonian, "row", axis=0, tiled=True)
    hp_product = product(hamiltonian_rows, density_strip) * pattern
    ph_product = product(density_rows, hamiltonian_strip) * pattern
    hp_strip = lax.all_gather(hp_product, "row", axis=0, tiled=True)
    ph_strip = lax.all_gather(ph_product, "row", axis=0, tiled=True)
    hp_rows = lax.all_gather(hp_product, "col", axis=1, tiled=True)
    php_product = product(density_rows, hp_strip) * pattern
    pph_product = product(density_rows, ph_strip) * pattern
    hpp_product = product(hp_rows, density_strip) * pattern
    gradient = pattern * (
        3.0 * (hp_product + ph_product) - 2.0 * (php_product + pph_product + hpp_product)
    )
    return (hp_product, php_product, gradient)


ROWS, COLS = 4, 8


def swap(x, axis, mask):
    size = ROWS if axis == "row" else COLS
    return lax.ppermute(x, axis, [(i, i ^ mask) for i in range(size)])


def after(value, *others):
    return lax.optimization_barrier((value, *others))[0]


def split(x):
    high = x.astype(jnp.bfloat16)
    return high, (x - high.astype(jnp.float32)).astype(jnp.bfloat16)


def stacked(x):
    return jnp.concatenate(split(x), axis=0)


def beside(x):
    return jnp.concatenate(split(x), axis=1)


def mul(a, b):
    return jnp.dot(a, b, preferred_element_type=jnp.float32)


def dot_parts(a, b):
    t = mul(a, b)
    m, n = t.shape[0] // 2, t.shape[1] // 2
    return (t[:m, :n] + (t[:m, n:] + t[m:, :n])) + t[m:, n:]


def dot_wide(a, b):
    t = mul(a, b[0])
    m = t.shape[0] // 2
    return t[:m] + (t[m:] + mul(a[:m], b[1]))


def dot_tall(a, b):
    t = mul(a[0], b)
    n = t.shape[1] // 2
    return t[:, :n] + (t[:, n:] + mul(a[1], b[:, :n]))


def place(r, col_block):
    band = jnp.bitwise_xor(lax.shift_right_logical(col_block, 1), r)
    start = band * (2 * BLK) + jnp.bitwise_and(col_block, 1) * BLK
    return pl.multiple_of(start, BLK)


def block_at(r, position):
    return 2 * jnp.bitwise_xor(position // 2, r) + position % 2


def pattern_of(mask_ref, row_blocks, col_blocks):
    rows = []
    for i in row_blocks:
        rows.append(
            jnp.concatenate(
                [jnp.full((BLK, BLK), mask_ref[i, j].astype(jnp.float32)) for j in col_blocks],
                axis=1,
            )
        )
    return jnp.concatenate(rows, axis=0)


def band_blocks(r, m):
    return [block_at(r, 2 * m), block_at(r, 2 * m + 1)]


BAND = 2 * BLK


def fill_rows(mask_ref, r, c, ss, so, first, out):
    for j in range(4):
        for flip, ref in ((0, ss), (1, so)):
            block = jnp.bitwise_xor(c, 2 * j + flip)
            part = ref[first + j] * pattern_of(mask_ref, band_blocks(r, 0), [block])
            out[:, pl.ds(place(r, block), BLK)] = stacked(part)


def fill_cols(mask_ref, r, c, parts, out):
    for m, part in enumerate(parts):
        kept = part * pattern_of(mask_ref, band_blocks(r, m), [c])
        out[m * BAND : (m + 1) * BAND, :] = beside(kept)


def left_pair(mask_ref, r, blocks, first, at):
    parts = [
        first[at + i] * pattern_of(mask_ref, band_blocks(r, 0), [blocks[i]]) for i in (0, 1)
    ]
    return stacked(jnp.concatenate(parts, axis=1))


def pairs(c, flip):
    for j in (0, 2):
        yield j, [jnp.bitwise_xor(c, 2 * (j + i) + flip) for i in (0, 1)]


def start_kernel(mask_ref, p0, p1, p3, p2, ss, part_ref, pcol):
    r, c = lax.axis_index("row"), lax.axis_index("col")
    fill_cols(mask_ref, r, c, (p0[...], p1[...], p2[...], p3[...]), pcol)
    total = jnp.zeros(part_ref.shape, jnp.float32)
    for j, blocks in pairs(c, 0):
        total += dot_parts(left_pair(mask_ref, r, blocks, ss, j), rows_at(r, pcol, blocks))
    part_ref[...] = total


def hp_kernel(mask_ref, part_ref, pcol, ss, so, send_ref, mark_ref):
    r, c = lax.axis_index("row"), lax.axis_index("col")
    total = part_ref[...]
    for j, blocks in pairs(c, 1):
        total += dot_parts(left_pair(mask_ref, r, blocks, so, j), rows_at(r, pcol, blocks))
    own = pattern_of(mask_ref, band_blocks(r, 0), [c])
    send_ref[0:BAND] = total * own
    send_ref[BAND:] = ss[0] * own
    mark_ref[...] = jnp.zeros_like(mark_ref)


def rows_kernel(mask_ref, ss, so, send_ref, mark_ref, hrow, prow, hp_ref):
    r, c = lax.axis_index("row"), lax.axis_index("col")
    hp_ref[...] = send_ref[0:BAND]
    fill_rows(mask_ref, r, c, ss, so, 0, hrow)
    fill_rows(mask_ref, r, c, ss, so, 4, prow)


def is_middle(r):
    return jnp.logical_or(r == 1, r == 2)


def column_pair(mask_ref, r, blocks, j, first, rest):
    bands = []
    for m in range(4):
        parts = []
        for i in (0, 1):
            part = first[4 + j + i] if m == 0 else rest[i, (m - 1) * BAND : m * BAND]
            parts.append(part * pattern_of(mask_ref, band_blocks(r, m), [blocks[i]]))
        bands.append(jnp.concatenate(parts, axis=1))
    return split(jnp.concatenate(bands, axis=0))


def rows_at(r, ref, blocks):
    return jnp.concatenate([ref[pl.ds(place(r, b), BLK), :] for b in blocks], axis=0)


def far_rows(cols):
    return jnp.concatenate([part[BAND : 2 * BAND] for part in cols], axis=0)


def h_kernel(mask_ref, q0, q1, q3, q2, hcol, across_ref):
    r, c = lax.axis_index("row"), lax.axis_index("col")
    fill_cols(mask_ref, r, c, [ref[BAND:] for ref in (q0, q1, q2, q3)], hcol)
    across_ref[0:BAND] = q3[0:BAND]
    across_ref[BAND:] = q2[0:BAND]


def any_live(mask_ref, blocks, c):
    return sum(mask_ref[b, c] for b in blocks) != 0


def add_ph(mask_ref, r, c, pair, first, rest, hcol, ph_ref, far):
    j, blocks = pair

    @pl.when(any_live(mask_ref, blocks, c))
    def _():
        cols = column_pair(mask_ref, r, blocks, j, first, rest)
        ph_ref[...] += dot_tall(cols, rows_at(r, hcol, blocks))
        far[...] = far_rows(cols)


def own_kernel(mask_ref, hcol, ss, lo, hi, ph_ref, far_lo, far_hi):
    r, c = lax.axis_index("row"), lax.axis_index("col")

    @pl.when(is_middle(r))
    def _():
        ph_ref[...] = jnp.zeros_like(ph_ref)
        for pair, rest, far in zip(pairs(c, 0), (lo, hi), (far_lo, far_hi)):
            add_ph(mask_ref, r, c, pair, ss, rest, hcol, ph_ref, far)


def other_kernel(mask_ref, hcol, so, hi, part_ref, ph_ref, far):
    r, c = lax.axis_index("row"), lax.axis_index("col")

    @pl.when(is_middle(r))
    def _():
        ph_ref[...] = part_ref[...]
        _, pair = pairs(c, 1)
        add_ph(mask_ref, r, c, pair, so, hi, hcol, ph_ref, far)


def ph_kernel(
    mask_ref, hcol, so, lo, part_ref, own_lo, own_hi, other_hi, back_ref, tile_ref, ph2,
    ph_ref, other_lo,
):
    r, c = lax.axis_index("row"), lax.axis_index("col")
    back_ref[...] = jnp.zeros_like(back_ref)
    tile_ref[...] = jnp.zeros_like(tile_ref)
    ph2[...] = jnp.zeros_like(ph2)

    @pl.when(is_middle(r))
    def _():
        ph_ref[...] = part_ref[...]
        add_ph(mask_ref, r, c, next(pairs(c, 1)), so, lo, hcol, ph_ref, other_lo)
        for m in range(4):
            at = pl.ds(m * BAND, BAND)
            rows = ph_ref[at, :] * pattern_of(mask_ref, band_blocks(r, m), [c])
            ph2[at, :] = beside(rows)
            if m == 0:
                tile_ref[...] = rows
            if m == 1:
                back_ref[...] = 3.0 * rows
        there = pattern_of(mask_ref, band_blocks(r, 1), [c])
        meets_c = any_live(mask_ref, band_blocks(r, 1), c)
        fars = ((0, (own_lo, own_hi)), (1, (other_lo, other_hi)))
        for flip, parts in fars:
            for (_, blocks), far in zip(pairs(c, flip), parts):

                met = [mask_ref[b, c] * any_live(mask_ref, band_blocks(r, 1), b).astype(jnp.int32) for b in blocks]

                @pl.when(jnp.logical_and(sum(met) != 0, meets_c))
                def _(blocks=blocks, far=far):
                    term = dot_parts(far[...], rows_at(r, ph2, blocks))
                    back_ref[...] -= 2.0 * there * term


def column(mask_ref, r, block, j, first, rest):
    bands = []
    for m in range(4):
        part = first[4 + j] if m == 0 else rest[j % 2, (m - 1) * BAND : m * BAND]
        bands.append(part * pattern_of(mask_ref, band_blocks(r, m), [block]))
    return beside(jnp.concatenate(bands, axis=0))


def last_kernel(
    mask_ref, prow, hrow, pcol, ss, so, s_lo, s_hi, o_lo, o_hi, ph2, send_ref, q1, q2, q3, q23,
    ph_ref, php_ref, grad_ref, qcol, acc,
):
    r, c = lax.axis_index("row"), lax.axis_index("col")
    own = pattern_of(mask_ref, band_blocks(r, 0), [c])
    hp = send_ref[0:BAND]

    for m, part in enumerate((hp, q1[0:BAND])):
        qcol[m * BAND : (m + 1) * BAND, :] = beside(part)

    @pl.when(is_middle(r))
    def _():
        for m, part in ((2, q2[0:BAND]), (3, q3[0:BAND])):
            qcol[m * BAND : (m + 1) * BAND, :] = beside(part)
        acc[...] = dot_parts(prow[...], ph2[...])

    @pl.when(jnp.logical_not(is_middle(r)))
    def _():
        for m, part in ((2, q23[0:BAND]), (3, q23[BAND:])):
            qcol[m * BAND : (m + 1) * BAND, :] = beside(part)
        acc[...] = jnp.zeros_like(acc)

    php = dot_parts(prow[...], qcol[...]) * own
    php_ref[...] = php
    acc[...] += dot_parts(stacked(hp), rows_at(r, pcol, [c]))
    for flip, first, rests in ((0, ss, (s_lo, s_hi)), (1, so, (o_lo, o_hi))):
        for j in range(1 - flip, 4):
            block = jnp.bitwise_xor(c, 2 * j + flip)

            met = any_live(mask_ref, band_blocks(r, 0), block)

            @pl.when(jnp.logical_and(mask_ref[block, c] != 0, met))
            def _(first=first, rest=rests[j // 2], j=j, block=block):
                cols = column(mask_ref, r, block, j, first, rest)
                rows = dot_parts(hrow[...], cols)
                rows = rows * pattern_of(mask_ref, band_blocks(r, 0), [block])
                acc[...] += dot_parts(stacked(rows), rows_at(r, pcol, [block]))

    grad_ref[...] = 3.0 * (hp + ph_ref[...]) - 2.0 * (php + own * acc[...])


def call(kernel, outs, scratch, flops, *args):
    smem, vmem = pl.BlockSpec(memory_space=pltpu.SMEM), pl.BlockSpec(memory_space=pltpu.VMEM)
    moved = sum(a.size * a.dtype.itemsize for a in (*args, *outs))
    return pl.pallas_call(
        kernel,
        out_shape=outs,
        in_specs=[smem] + [vmem] * (len(args) - 1),
        out_specs=tuple(vmem for _ in outs),
        scratch_shapes=scratch,
        cost_estimate=pl.CostEstimate(flops=flops, bytes_accessed=moved, transcendentals=0),
        compiler_params=pltpu.CompilerParams(vmem_limit_bytes=VMEM_LIMIT),
    )(*args)


def to_middle(x):
    routes = [
        [(0, 1), (3, 2), (1, 0), (2, 3)],
        [(0, 2), (3, 1), (1, 0), (2, 3)],
        [(1, 2), (2, 1), (0, 0), (3, 3)],
    ]
    return [lax.ppermute(x, "row", pairs) for pairs in routes]


def whole_body(density, hamiltonian, block_mask):
    f32, bf16 = jnp.float32, jnp.bfloat16
    rows, cols = density.shape
    order = rows * ROWS

    def shape(a, b, dtype=bf16):
        return jax.ShapeDtypeStruct((a, b), dtype)

    tile, strip = shape(rows, cols, f32), shape(order, cols, f32)
    rows2, cols2 = shape(2 * rows, order), shape(order, 2 * cols)
    weight = 6 * rows * order * order
    p0, h0 = density, hamiltonian
    hx, py = swap(h0, "col", 2), swap(p0, "col", 4)
    p3 = swap(p0, "row", 3)
    both = lax.optimization_barrier(jnp.concatenate([p0, h0], axis=0))
    p0, h0 = both[:rows], both[rows:]
    p1 = swap(p0, "row", 1)
    p2 = swap(p0, "row", 2)
    hy = swap(jnp.concatenate([h0, hx], axis=0), "col", 4)
    px = swap(jnp.concatenate([p0, py], axis=0), "col", 2)
    px, p1, hy, p2, p3 = lax.optimization_barrier((px, p1, hy, p2, p3))
    ss = jnp.stack([h0, hx, hy[:rows], hy[rows:], p0, px[:rows], py, px[rows:]])
    so = swap(ss, "col", 1)

    b = jnp.concatenate([p1, p2, p3], axis=0)
    half = b.shape[0] // 2
    upper, lower = b[:half], b[half:]
    ux, ly = swap(upper, "col", 2), swap(lower, "col", 4)

    part, pcol = call(start_kernel, (tile, cols2), [], weight, block_mask, p0, p1, p3, p2, ss)
    send, mark = call(
        hp_kernel, (shape(2 * rows, cols, f32), shape(8, cols, f32)), [], weight,
        block_mask, part, pcol, ss, so,
    )
    ly, ux, mark = lax.optimization_barrier((ly, ux, mark))
    q1, q2, q3 = to_middle(send)
    uy = swap(jnp.concatenate([upper, ux], axis=0), "col", 4)
    lx = swap(jnp.concatenate([lower, ly], axis=0), "col", 2)
    hrow, prow, hp = call(
        rows_kernel, (rows2, rows2, tile), [], weight, block_mask, ss, so, send, mark
    )
    hcol, across = call(
        h_kernel, (cols2, shape(2 * rows, cols, f32)), [], AHEAD * weight,
        block_mask, send, q1, q3, q2,
    )
    q23 = swap(across, "row", 1)
    lx, uy, hcol = lax.optimization_barrier((lx, uy, hcol))
    s_lo = jnp.stack([b, jnp.concatenate([ux, lx[:half]], axis=0)])
    s_hi = jnp.stack([jnp.concatenate(pair, axis=0) for pair in ((uy[:half], ly), (uy[half:], lx[half:]))])
    o_lo, o_hi = swap(s_lo, "col", 1), swap(s_hi, "col", 1)

    far = shape(2 * rows, order // 4)
    part, own_lo, own_hi = call(
        own_kernel, (strip, far, far), [], AHEAD * weight, block_mask, hcol, ss, s_lo, s_hi
    )
    part, other_hi = call(
        other_kernel, (strip, far), [], weight, block_mask, hcol, so, o_hi, part
    )
    back, ph, ph2 = call(
        ph_kernel, (tile, tile, cols2),
        [pltpu.VMEM((order, cols), f32), pltpu.VMEM((2 * rows, order // 4), bf16)], weight,
        block_mask, hcol, so, o_lo, part, own_lo, own_hi, other_hi,
    )
    got = swap(back, "row", 1)
    php, grad = call(
        last_kernel, (tile, tile),
        [pltpu.VMEM((order, 2 * cols), bf16), pltpu.VMEM((rows, cols), f32)], weight,
        block_mask, prow, hrow, pcol, ss, so, s_lo, s_hi, o_lo, o_hi, ph2, send, q1, q2, q3, q23,
        ph,
    )
    return hp, php, grad + got


def body(density, hamiltonian, block_mask, shape):
    tile_rows, tile_cols = density.shape
    if shape == (ROWS, COLS) and tile_rows == 2 * BLK and tile_cols == BLK:
        return whole_body(density, hamiltonian, block_mask)
    return strips_body(density, hamiltonian, block_mask)


def solution(mesh):
    placed = (P("row", "col"), P("row", "col"), P())
    return jax.shard_map(
        functools.partial(body, shape=(mesh.shape["row"], mesh.shape["col"])),
        mesh=mesh,
        in_specs=placed,
        out_specs=(P("row", "col"), P("row", "col"), P("row", "col")),
        check_vma=False,
    )
```

```python
import functools

import jax
import jax.numpy as jnp
from jax import lax
from jax.experimental import pallas as pl
from jax.experimental.pallas import tpu as pltpu
from jax.sharding import PartitionSpec as P

BLK = 128
VMEM_LIMIT = 40 * 1024 * 1024
AHEAD = 8

highest = lax.Precision.HIGHEST


def product(leading, second):
    return jnp.dot(leading, second, precision=highest, preferred_element_type=jnp.float32)


def tile_pattern(block_mask, row_index, col_index, tile_rows, tile_cols):
    row_blocks = (row_index * tile_rows + jnp.arange(tile_rows, dtype=jnp.int32)) // BLK
    col_blocks = (col_index * tile_cols + jnp.arange(tile_cols, dtype=jnp.int32)) // BLK
    block_ids = jnp.arange(block_mask.shape[0], dtype=jnp.int32)
    row_hot = (row_blocks[:, None] == block_ids[None, :]).astype(jnp.float32)
    col_hot = (col_blocks[:, None] == block_ids[None, :]).astype(jnp.float32)
    return product(product(row_hot, block_mask.astype(jnp.float32)), col_hot.T)


def strips_body(density, hamiltonian, block_mask):
    row_index = lax.axis_index("row")
    col_index = lax.axis_index("col")
    pattern = tile_pattern(block_mask, row_index, col_index, *density.shape)
    kept_density = density * pattern
    kept_hamiltonian = hamiltonian * pattern
    density_rows = lax.all_gather(kept_density, "col", axis=1, tiled=True)
    hamiltonian_rows = lax.all_gather(kept_hamiltonian, "col", axis=1, tiled=True)
    density_strip = lax.all_gather(kept_density, "row", axis=0, tiled=True)
    hamiltonian_strip = lax.all_gather(kept_hamiltonian, "row", axis=0, tiled=True)
    hp_product = product(hamiltonian_rows, density_strip) * pattern
    ph_product = product(density_rows, hamiltonian_strip) * pattern
    hp_strip = lax.all_gather(hp_product, "row", axis=0, tiled=True)
    ph_strip = lax.all_gather(ph_product, "row", axis=0, tiled=True)
    hp_rows = lax.all_gather(hp_product, "col", axis=1, tiled=True)
    php_product = product(density_rows, hp_strip) * pattern
    pph_product = product(density_rows, ph_strip) * pattern
    hpp_product = product(hp_rows, density_strip) * pattern
    gradient = pattern * (
        3.0 * (hp_product + ph_product) - 2.0 * (php_product + pph_product + hpp_product)
    )
    return (hp_product, php_product, gradient)


ROWS, COLS = 4, 8


def swap(x, axis, mask):
    size = ROWS if axis == "row" else COLS
    return lax.ppermute(x, axis, [(i, i ^ mask) for i in range(size)])


def after(value, *others):
    return lax.optimization_barrier((value, *others))[0]


def split(x):
    high = x.astype(jnp.bfloat16)
    return high, (x - high.astype(jnp.float32)).astype(jnp.bfloat16)


def stacked(x):
    return jnp.concatenate(split(x), axis=0)


def beside(x):
    return jnp.concatenate(split(x), axis=1)


def mul(a, b):
    return jnp.dot(a, b, preferred_element_type=jnp.float32)


def dot_parts(a, b):
    t = mul(a, b)
    m, n = t.shape[0] // 2, t.shape[1] // 2
    return (t[:m, :n] + (t[:m, n:] + t[m:, :n])) + t[m:, n:]


def dot_wide(a, b):
    t = mul(a, b[0])
    m = t.shape[0] // 2
    return t[:m] + (t[m:] + mul(a[:m], b[1]))


def dot_tall(a, b):
    t = mul(a[0], b)
    n = t.shape[1] // 2
    return t[:, :n] + (t[:, n:] + mul(a[1], b[:, :n]))


def place(r, col_block):
    band = jnp.bitwise_xor(lax.shift_right_logical(col_block, 1), r)
    start = band * (2 * BLK) + jnp.bitwise_and(col_block, 1) * BLK
    return pl.multiple_of(start, BLK)


def block_at(r, position):
    return 2 * jnp.bitwise_xor(position // 2, r) + position % 2


def pattern_of(mask_ref, row_blocks, col_blocks):
    rows = []
    for i in row_blocks:
        rows.append(
            jnp.concatenate(
                [jnp.full((BLK, BLK), mask_ref[i, j].astype(jnp.float32)) for j in col_blocks],
                axis=1,
            )
        )
    return jnp.concatenate(rows, axis=0)


def band_blocks(r, m):
    return [block_at(r, 2 * m), block_at(r, 2 * m + 1)]


BAND = 2 * BLK


def fill_rows(mask_ref, r, c, ss, so, first, out):
    for j in range(4):
        for flip, ref in ((0, ss), (1, so)):
            block = jnp.bitwise_xor(c, 2 * j + flip)
            part = ref[first + j] * pattern_of(mask_ref, band_blocks(r, 0), [block])
            out[:, pl.ds(place(r, block), BLK)] = stacked(part)


def fill_cols(mask_ref, r, c, parts, out):
    for m, part in enumerate(parts):
        kept = part * pattern_of(mask_ref, band_blocks(r, m), [c])
        out[m * BAND : (m + 1) * BAND, :] = beside(kept)


def left_pair(mask_ref, r, blocks, first, at):
    parts = [
        first[at + i] * pattern_of(mask_ref, band_blocks(r, 0), [blocks[i]]) for i in (0, 1)
    ]
    return stacked(jnp.concatenate(parts, axis=1))


def pairs(c, flip):
    for j in (0, 2):
        yield j, [jnp.bitwise_xor(c, 2 * (j + i) + flip) for i in (0, 1)]


def start_kernel(mask_ref, p0, p1, p3, p2, ss, part_ref, pcol):
    r, c = lax.axis_index("row"), lax.axis_index("col")
    fill_cols(mask_ref, r, c, (p0[...], p1[...], p2[...], p3[...]), pcol)
    total = jnp.zeros(part_ref.shape, jnp.float32)
    for j, blocks in pairs(c, 0):
        total += dot_parts(left_pair(mask_ref, r, blocks, ss, j), rows_at(r, pcol, blocks))
    part_ref[...] = total


def hp_kernel(mask_ref, part_ref, pcol, ss, so, send_ref, mark_ref):
    r, c = lax.axis_index("row"), lax.axis_index("col")
    send_ref[0:BAND] = part_ref[...]
    for j, blocks in pairs(c, 1):

        @pl.when(any_live(mask_ref, blocks, c))
        def _(j=j, blocks=blocks):
            left = left_pair(mask_ref, r, blocks, so, j)
            send_ref[0:BAND] += dot_parts(left, rows_at(r, pcol, blocks))

    own = pattern_of(mask_ref, band_blocks(r, 0), [c])
    send_ref[0:BAND] = send_ref[0:BAND] * own
    send_ref[BAND:] = ss[0] * own
    mark_ref[...] = jnp.zeros_like(mark_ref)


def rows_kernel(mask_ref, ss, so, send_ref, mark_ref, hrow, prow, hp_ref):
    r, c = lax.axis_index("row"), lax.axis_index("col")
    hp_ref[...] = send_ref[0:BAND]
    fill_rows(mask_ref, r, c, ss, so, 0, hrow)
    fill_rows(mask_ref, r, c, ss, so, 4, prow)


def is_middle(r):
    return jnp.logical_or(r == 1, r == 2)


def column_pair(mask_ref, r, blocks, j, first, rest):
    bands = []
    for m in range(4):
        parts = []
        for i in (0, 1):
            part = first[4 + j + i] if m == 0 else rest[i, (m - 1) * BAND : m * BAND]
            parts.append(part * pattern_of(mask_ref, band_blocks(r, m), [blocks[i]]))
        bands.append(jnp.concatenate(parts, axis=1))
    return split(jnp.concatenate(bands, axis=0))


def rows_at(r, ref, blocks):
    return jnp.concatenate([ref[pl.ds(place(r, b), BLK), :] for b in blocks], axis=0)


def far_rows(cols):
    return jnp.concatenate([part[BAND : 2 * BAND] for part in cols], axis=0)


def h_kernel(mask_ref, q0, q1, q3, q2, hcol, across_ref):
    r, c = lax.axis_index("row"), lax.axis_index("col")
    fill_cols(mask_ref, r, c, [ref[BAND:] for ref in (q0, q1, q2, q3)], hcol)
    across_ref[0:BAND] = q3[0:BAND]
    across_ref[BAND:] = q2[0:BAND]


def any_live(mask_ref, blocks, c):
    return sum(mask_ref[b, c] for b in blocks) != 0


def add_ph(mask_ref, r, c, pair, first, rest, hcol, ph_ref, far):
    j, blocks = pair

    @pl.when(any_live(mask_ref, blocks, c))
    def _():
        cols = column_pair(mask_ref, r, blocks, j, first, rest)
        ph_ref[...] += dot_tall(cols, rows_at(r, hcol, blocks))
        far[...] = far_rows(cols)


def own_kernel(mask_ref, hcol, ss, lo, hi, ph_ref, far_lo, far_hi):
    r, c = lax.axis_index("row"), lax.axis_index("col")

    @pl.when(is_middle(r))
    def _():
        ph_ref[...] = jnp.zeros_like(ph_ref)
        for pair, rest, far in zip(pairs(c, 0), (lo, hi), (far_lo, far_hi)):
            add_ph(mask_ref, r, c, pair, ss, rest, hcol, ph_ref, far)


def other_kernel(mask_ref, hcol, so, hi, part_ref, ph_ref, far):
    r, c = lax.axis_index("row"), lax.axis_index("col")

    @pl.when(is_middle(r))
    def _():
        ph_ref[...] = part_ref[...]
        _, pair = pairs(c, 1)
        add_ph(mask_ref, r, c, pair, so, hi, hcol, ph_ref, far)


def ph_kernel(
    mask_ref, hcol, so, lo, part_ref, own_lo, own_hi, other_hi, back_ref, tile_ref, ph2,
    ph_ref, other_lo,
):
    r, c = lax.axis_index("row"), lax.axis_index("col")
    back_ref[...] = jnp.zeros_like(back_ref)
    tile_ref[...] = jnp.zeros_like(tile_ref)
    ph2[...] = jnp.zeros_like(ph2)

    @pl.when(is_middle(r))
    def _():
        ph_ref[...] = part_ref[...]
        add_ph(mask_ref, r, c, next(pairs(c, 1)), so, lo, hcol, ph_ref, other_lo)
        for m in range(4):
            at = pl.ds(m * BAND, BAND)
            rows = ph_ref[at, :] * pattern_of(mask_ref, band_blocks(r, m), [c])
            ph2[at, :] = beside(rows)
            if m == 0:
                tile_ref[...] = rows
            if m == 1:
                back_ref[...] = 3.0 * rows
        there = pattern_of(mask_ref, band_blocks(r, 1), [c])
        fars = ((0, (own_lo, own_hi)), (1, (other_lo, other_hi)))
        for flip, parts in fars:
            for (_, blocks), far in zip(pairs(c, flip), parts):

                @pl.when(any_live(mask_ref, blocks, c))
                def _(blocks=blocks, far=far):
                    term = dot_parts(far[...], rows_at(r, ph2, blocks))
                    back_ref[...] -= 2.0 * there * term


def column(mask_ref, r, block, j, first, rest):
    bands = []
    for m in range(4):
        part = first[4 + j] if m == 0 else rest[j % 2, (m - 1) * BAND : m * BAND]
        bands.append(part * pattern_of(mask_ref, band_blocks(r, m), [block]))
    return beside(jnp.concatenate(bands, axis=0))


def last_kernel(
    mask_ref, prow, hrow, pcol, ss, so, s_lo, s_hi, o_lo, o_hi, ph2, send_ref, q1, q2, q3, q23,
    ph_ref, php_ref, grad_ref, qcol, acc,
):
    r, c = lax.axis_index("row"), lax.axis_index("col")
    own = pattern_of(mask_ref, band_blocks(r, 0), [c])
    hp = send_ref[0:BAND]

    for m, part in enumerate((hp, q1[0:BAND])):
        qcol[m * BAND : (m + 1) * BAND, :] = beside(part)

    @pl.when(is_middle(r))
    def _():
        for m, part in ((2, q2[0:BAND]), (3, q3[0:BAND])):
            qcol[m * BAND : (m + 1) * BAND, :] = beside(part)
        acc[...] = dot_parts(prow[...], ph2[...])

    @pl.when(jnp.logical_not(is_middle(r)))
    def _():
        for m, part in ((2, q23[0:BAND]), (3, q23[BAND:])):
            qcol[m * BAND : (m + 1) * BAND, :] = beside(part)
        acc[...] = jnp.zeros_like(acc)

    php = dot_parts(prow[...], qcol[...]) * own
    php_ref[...] = php
    acc[...] += dot_parts(stacked(hp), rows_at(r, pcol, [c]))
    for flip, first, rests in ((0, ss, (s_lo, s_hi)), (1, so, (o_lo, o_hi))):
        for j in range(1 - flip, 4):
            block = jnp.bitwise_xor(c, 2 * j + flip)

            met = any_live(mask_ref, band_blocks(r, 0), block)

            @pl.when(jnp.logical_and(mask_ref[block, c] != 0, met))
            def _(first=first, rest=rests[j // 2], j=j, block=block):
                cols = column(mask_ref, r, block, j, first, rest)
                rows = dot_parts(hrow[...], cols)
                rows = rows * pattern_of(mask_ref, band_blocks(r, 0), [block])
                acc[...] += dot_parts(stacked(rows), rows_at(r, pcol, [block]))

    grad_ref[...] = 3.0 * (hp + ph_ref[...]) - 2.0 * (php + own * acc[...])


def call(kernel, outs, scratch, flops, *args):
    smem, vmem = pl.BlockSpec(memory_space=pltpu.SMEM), pl.BlockSpec(memory_space=pltpu.VMEM)
    moved = sum(a.size * a.dtype.itemsize for a in (*args, *outs))
    return pl.pallas_call(
        kernel,
        out_shape=outs,
        in_specs=[smem] + [vmem] * (len(args) - 1),
        out_specs=tuple(vmem for _ in outs),
        scratch_shapes=scratch,
        cost_estimate=pl.CostEstimate(flops=flops, bytes_accessed=moved, transcendentals=0),
        compiler_params=pltpu.CompilerParams(vmem_limit_bytes=VMEM_LIMIT),
    )(*args)


def to_middle(x):
    routes = [
        [(0, 1), (3, 2), (1, 0), (2, 3)],
        [(0, 2), (3, 1), (1, 0), (2, 3)],
        [(1, 2), (2, 1), (0, 0), (3, 3)],
    ]
    return [lax.ppermute(x, "row", pairs) for pairs in routes]


def whole_body(density, hamiltonian, block_mask):
    f32, bf16 = jnp.float32, jnp.bfloat16
    rows, cols = density.shape
    order = rows * ROWS

    def shape(a, b, dtype=bf16):
        return jax.ShapeDtypeStruct((a, b), dtype)

    tile, strip = shape(rows, cols, f32), shape(order, cols, f32)
    rows2, cols2 = shape(2 * rows, order), shape(order, 2 * cols)
    weight = 6 * rows * order * order
    p0, h0 = density, hamiltonian
    hx, py = swap(h0, "col", 2), swap(p0, "col", 4)
    p3 = swap(p0, "row", 3)
    both = lax.optimization_barrier(jnp.concatenate([p0, h0], axis=0))
    p0, h0 = both[:rows], both[rows:]
    p1 = swap(p0, "row", 1)
    p2 = swap(p0, "row", 2)
    hy = swap(jnp.concatenate([h0, hx], axis=0), "col", 4)
    px = swap(jnp.concatenate([p0, py], axis=0), "col", 2)
    px, p1, hy, p2, p3 = lax.optimization_barrier((px, p1, hy, p2, p3))
    ss = jnp.stack([h0, hx, hy[:rows], hy[rows:], p0, px[:rows], py, px[rows:]])
    so = swap(ss, "col", 1)

    b = jnp.concatenate([p1, p2, p3], axis=0)
    half = b.shape[0] // 2
    upper, lower = b[:half], b[half:]
    ux, ly = swap(upper, "col", 2), swap(lower, "col", 4)

    part, pcol = call(start_kernel, (tile, cols2), [], weight, block_mask, p0, p1, p3, p2, ss)
    send, mark = call(
        hp_kernel, (shape(2 * rows, cols, f32), shape(8, cols, f32)), [], weight,
        block_mask, part, pcol, ss, so,
    )
    ly, ux, mark = lax.optimization_barrier((ly, ux, mark))
    q1, q2, q3 = to_middle(send)
    uy = swap(jnp.concatenate([upper, ux], axis=0), "col", 4)
    lx = swap(jnp.concatenate([lower, ly], axis=0), "col", 2)
    hrow, prow, hp = call(
        rows_kernel, (rows2, rows2, tile), [], weight, block_mask, ss, so, send, mark
    )
    hcol, across = call(
        h_kernel, (cols2, shape(2 * rows, cols, f32)), [], AHEAD * weight,
        block_mask, send, q1, q3, q2,
    )
    q23 = swap(across, "row", 1)
    lx, uy, hcol = lax.optimization_barrier((lx, uy, hcol))
    s_lo = jnp.stack([b, jnp.concatenate([ux, lx[:half]], axis=0)])
    s_hi = jnp.stack([jnp.concatenate(pair, axis=0) for pair in ((uy[:half], ly), (uy[half:], lx[half:]))])
    o_lo, o_hi = swap(s_lo, "col", 1), swap(s_hi, "col", 1)

    far = shape(2 * rows, order // 4)
    part, own_lo, own_hi = call(
        own_kernel, (strip, far, far), [], AHEAD * weight, block_mask, hcol, ss, s_lo, s_hi
    )
    part, other_hi = call(
        other_kernel, (strip, far), [], weight, block_mask, hcol, so, o_hi, part
    )
    back, ph, ph2 = call(
        ph_kernel, (tile, tile, cols2),
        [pltpu.VMEM((order, cols), f32), pltpu.VMEM((2 * rows, order // 4), bf16)], weight,
        block_mask, hcol, so, o_lo, part, own_lo, own_hi, other_hi,
    )
    got = swap(back, "row", 1)
    php, grad = call(
        last_kernel, (tile, tile),
        [pltpu.VMEM((order, 2 * cols), bf16), pltpu.VMEM((rows, cols), f32)], weight,
        block_mask, prow, hrow, pcol, ss, so, s_lo, s_hi, o_lo, o_hi, ph2, send, q1, q2, q3, q23,
        ph,
    )
    return hp, php, grad + got


def body(density, hamiltonian, block_mask, shape):
    tile_rows, tile_cols = density.shape
    if shape == (ROWS, COLS) and tile_rows == 2 * BLK and tile_cols == BLK:
        return whole_body(density, hamiltonian, block_mask)
    return strips_body(density, hamiltonian, block_mask)


def solution(mesh):
    placed = (P("row", "col"), P("row", "col"), P())
    return jax.shard_map(
        functools.partial(body, shape=(mesh.shape["row"], mesh.shape["col"])),
        mesh=mesh,
        in_specs=placed,
        out_specs=(P("row", "col"), P("row", "col"), P("row", "col")),
        check_vma=False,
    )
```
